32 devices in a mesh: section: 16 (over z, y, x), rep: 2 (over core).
Axes of the slice: x: 2, y: 2, z: 4, core: 2. Of those that a mesh axis runs over, the one named last changes fastest.
Arguments:
- features: bfloat16 [4096, 512], P(('section', 'rep')), may hold values from -6 to 6
- col_panels: int32 [32, 2, 12], P('section', 'rep'), may hold values from 0 to 31, as said below
- block_counts: int32 [32, 2], P('section', 'rep'), may hold values from 1 to 12, as said below
- block_values: bfloat16 [32, 2, 12, 128, 128], P('section', 'rep'), may hold values from 0.0019989014 to 0.019897461
- weight: bfloat16 [512, 512], replicated, may hold values from -0.25 to 0.25
- bias: float32 [512], replicated, may hold values from -3 to 3
- cotangent: bfloat16 [4096, 512], P(('section', 'rep')), may hold values from -6 to 6
Outputs:
- hidden: bfloat16 [4096, 512], P(('section', 'rep'))
- weight_grad: float32 [512, 512], replicated
- bias_grad: float32 [512], replicated
The draws below stay inside these ranges and needn't reach their ends.
Inputs may be any that keep to these rules, and one draw needn't show every extreme that they name: Column group r holds the column panels c with (c) % 2 == r; col_panels[p, r, k] lies in column group r, and the 12 entries of one list are distinct. Only the first block_counts[p, r] slots of a list are nonzero blocks; later slots are ignored. The count 12 occurs in every draw.
All inputs are finite; a program needn't handle non-finite values.
Results may differ from the reference program's by a relative error of at most 0.0055.
Values may be sent and summed in bfloat16 or wider, within the bound.
A program may use at most 64 MiB of HBM per device.

```python
import math
import jax
import jax.numpy as jnp
from jax import lax

BLOCK = 128
WIDTH = 512
PANELS_DEV = 1
REPS = 2
GROUP = 2
PANELS = 32
NODES = 4096
COLUMNS = 16
SLOTS = 12


def draw_col_panels(key, part):
    scores = jax.random.randint(key, (PANELS, REPS, COLUMNS), 0, 1 << 20) * COLUMNS
    scores = scores + jnp.arange(COLUMNS, dtype=jnp.int32)
    order = jnp.argsort(scores, axis=-1)[..., :SLOTS].astype(jnp.int32)
    section_part = order // PANELS_DEV
    within = order % PANELS_DEV
    rep_ids = jnp.arange(REPS, dtype=jnp.int32)[None, :, None]
    return ((section_part * REPS + rep_ids) * PANELS_DEV + within).astype(jnp.int32)


def draw_block_counts(key, part):
    first_key, second_key, third_key = jax.random.split(key, 3)
    section_count = PANELS // GROUP
    levels = jax.random.randint(first_key, (section_count, 1, 1), max(1, SLOTS // 4), SLOTS + 1)
    levels = jnp.broadcast_to(levels, (section_count, GROUP, REPS)).reshape(PANELS, REPS)
    counts = jax.random.randint(second_key, (PANELS, REPS), 1, levels + 1)
    forced = jax.random.randint(third_key, (), 0, PANELS)
    row_ids = jnp.arange(PANELS, dtype=jnp.int32)[:, None]
    return jnp.where(row_ids == forced, SLOTS, counts).astype(jnp.int32)


def block_scale(rng, dims, pieces, least, high):
    def one(dim, shards_of):
        draws = jax.random.uniform(jax.random.fold_in(jax.random.fold_in(rng, 6), dim), (shards_of,), jnp.float32, least / len(pieces), high / len(pieces))
        return jnp.repeat(jnp.exp(draws), dims[dim] // shards_of).reshape((-1,) + (1,) * (len(dims) - dim - 1))

    factor_of = one(*pieces[0])
    for cut in pieces[1:]:
        factor_of = factor_of * one(*cut)
    return factor_of


def gaussian(key, shape, width, most, cuts=(), kind=jnp.bfloat16):
    gain = block_scale(key, shape, cuts, -0.22, 0.18) if cuts else 1.0
    result = jax.random.normal(key, shape, jnp.float32) * width * gain
    return jnp.minimum(jnp.maximum(result, -most), most).astype(kind)


def setup_inputs(seed: int = 0) -> dict:
    key_of = jax.random.split(jax.random.key(seed), 8)
    features = gaussian(key_of[0], (NODES, WIDTH), 1.0, 6.0, ((0, 32),))
    col_panels = draw_col_panels(jax.random.fold_in(key_of[7], 71), 0)
    block_counts = draw_block_counts(jax.random.fold_in(key_of[7], 71), 0)
    block_values = jnp.clip(jnp.exp(math.log(0.019897461) - 2.2979944 * jax.random.uniform(key_of[3], (PANELS, REPS, SLOTS, BLOCK, BLOCK), jnp.float32) ** block_scale(key_of[3], (PANELS, REPS, SLOTS, BLOCK, BLOCK), ((0, 16), (1, 2)), -0.2, 0.2)), 0.0019989014, 0.019897461).astype(jnp.bfloat16)
    weight = gaussian(key_of[4], (WIDTH, WIDTH), WIDTH ** -0.5, 0.25)
    bias = gaussian(key_of[5], (WIDTH,), 0.5, 3.0, (), jnp.float32)
    cotangent = gaussian(key_of[6], (NODES, WIDTH), 1.0, 6.0, ((0, 32),))
    return dict(features=features, col_panels=col_panels, block_counts=block_counts, block_values=block_values, weight=weight, bias=bias, cotangent=cotangent)


def reference(features, col_panels, block_counts, block_values, weight, bias, cotangent):
    panel_feats = features.reshape(PANELS, BLOCK, WIDTH)
    slot_ids = jnp.arange(SLOTS, dtype=jnp.int32)

    def one_row(panel):
        column_ids = col_panels[panel].reshape(-1).astype(jnp.int32)
        live = (slot_ids[None, :] < block_counts[panel][:, None]).reshape(-1)
        tiles = block_values[panel].reshape(REPS * SLOTS, BLOCK, BLOCK).astype(jnp.float32)
        tiles = tiles * live[:, None, None].astype(jnp.float32)
        picked = panel_feats[column_ids].astype(jnp.float32)
        return jnp.einsum('kab,kbf->af', tiles, picked, precision=lax.Precision.HIGHEST)
    rows = lax.map(one_row, jnp.arange(PANELS, dtype=jnp.int32))
    aggregated = rows.reshape(NODES, WIDTH).astype(jnp.bfloat16)
    pre = jnp.dot(aggregated, weight, preferred_element_type=jnp.float32) + bias
    hidden = jax.nn.silu(pre).astype(jnp.bfloat16)
    sigmoid_pre = jax.nn.sigmoid(pre)
    slope = (cotangent.astype(jnp.float32) * (sigmoid_pre * (1.0 + pre * (1.0 - sigmoid_pre)))).astype(jnp.bfloat16)
    factor = 1.0 / math.sqrt(NODES)
    weight_grad = jnp.dot(aggregated.T, slope, preferred_element_type=jnp.float32) * factor
    bias_grad = lax.optimization_barrier(jnp.sum(slope.astype(jnp.float32), axis=0)) * factor
    return (hidden, weight_grad, bias_grad)
```

```python
import math

import jax
import jax.numpy as jnp
from jax import lax
from jax.experimental import pallas as pl
from jax.experimental.pallas import tpu as pltpu
from jax.sharding import PartitionSpec as P


def shards(features, col_panels, block_counts, block_values, weight, bias, cotangent):
    rep_count = lax.axis_size("rep")
    rep_index = lax.axis_index("rep")
    tile_size = block_values.shape[-1]
    feat_width = features.shape[1]
    own_panels = features.shape[0] // tile_size
    row_panels = col_panels.shape[0]
    slot_count = col_panels.shape[2]
    global_cols = col_panels[:, 0, :]
    local_cols = global_cols // (own_panels * rep_count) * own_panels + global_cols % own_panels
    live_counts = block_counts[:, 0]
    slot_mask = jnp.arange(slot_count, dtype=jnp.int32)[None, :] < live_counts[:, None]
    tiles = block_values[:, 0]
    empty = jnp.zeros((row_panels, tile_size, feat_width), jnp.float32)
    gathered = lax.all_gather(features, "section", axis=0, tiled=True)
    all_panels = gathered.reshape(-1, tile_size, feat_width)
    slot_step = 4
    turn_count = (jnp.max(live_counts) + slot_step - 1) // slot_step

    def one_turn(turn, running):
        begin_slot = turn * slot_step
        step_cols = lax.dynamic_slice_in_dim(local_cols, begin_slot, slot_step, 1)
        step_mask = lax.dynamic_slice_in_dim(slot_mask, begin_slot, slot_step, 1)
        step_tiles = lax.dynamic_slice_in_dim(tiles, begin_slot, slot_step, 1)
        step_tiles = jnp.where(step_mask[:, :, None, None], step_tiles, jnp.zeros((), jnp.bfloat16))
        picked = all_panels[step_cols]
        return running + jnp.einsum(
            "gkab,gkbf->gaf", step_tiles, picked, preferred_element_type=jnp.float32
        )

    gathered_sum = lax.fori_loop(0, turn_count, one_turn, empty)
    partial_value = gathered_sum.reshape(row_panels * tile_size, feat_width)
    own_rows = own_panels * tile_size
    summed_all = lax.psum(partial_value, "rep")
    summed_own = lax.dynamic_slice_in_dim(summed_all, rep_index * own_rows, own_rows, 0)
    aggregated = summed_own.astype(jnp.bfloat16)
    pre = jnp.dot(aggregated, weight, preferred_element_type=jnp.float32) + bias
    hidden = jax.nn.silu(pre).astype(jnp.bfloat16)
    sigmoid_pre = jax.nn.sigmoid(pre)
    slope = (
        cotangent.astype(jnp.float32) * (sigmoid_pre * (1.0 + pre * (1.0 - sigmoid_pre)))
    ).astype(jnp.bfloat16)
    local_weight = jnp.einsum("nd,nf->df", aggregated, slope, preferred_element_type=jnp.float32)
    local_bias = jnp.sum(slope.astype(jnp.float32), axis=0)
    weight_sum, bias_sum = lax.psum((local_weight, local_bias), ("section", "rep"))
    node_total = lax.axis_size("section") * rep_count * own_rows
    factor = 1.0 / math.sqrt(node_total)
    return (hidden, weight_sum * factor, bias_sum * factor)

MESH = pl.DeviceIdType.MESH
Z, PLANE = 4, 4


def fused_kernel(
    feat, cols, counts, blocks, weight, bias, cot,
    hid_out, wg_out, bias_out,
    gath, dense, blk, wv, cotv, acc_own, acc_oth, acc_in, aggs, hidv,
    pair_out, pair_in, half32, half16, plane_in, sum32, sum16, line_in, fin,
    ext, ext_pair, ext_plane, ext_line,
    loc_sem, z_s, z_r, x_s, x_r, y_s, y_r, dx_s, dx_r, dy_s, dy_r,
    p_s, p_r, rs_s, rs_r, zl_s, zl_r, zg_s, zg_r, pg_s, pg_r, cg_s, cg_r,
):
    tile, width = feat.shape
    slots = cols.shape[2]
    me, rep = lax.axis_index("section"), lax.axis_index("rep")
    z, q = me // PLANE, me % PLANE
    y, x = q // 2, q % 2

    def flip(j):
        return (1 - y if j & 2 else y) * 2 + (1 - x if j & 1 else x)

    def line(d):
        return lax.rem(z + d, Z)

    plane_peer = {j: (z * PLANE + flip(j), rep) for j in (1, 2, 3)}
    line_peer = {d: (line(d) * PLANE + q, rep) for d in (1, 2, 3)}
    core_peer = (me, 1 - rep)

    def remote(src, dst, send, recv, peer):
        return pltpu.make_async_remote_copy(
            src_ref=src, dst_ref=dst, send_sem=send, recv_sem=recv,
            device_id=peer, device_id_type=MESH,
        )

    own = gath.at[0, pl.ds(0, tile)]
    load_feat = pltpu.make_async_copy(feat, own, loc_sem.at[0])
    load_blk = pltpu.make_async_copy(blocks, blk, loc_sem.at[1])
    load_w = pltpu.make_async_copy(weight, wv, loc_sem.at[2])
    load_cot = pltpu.make_async_copy(cot, cotv, loc_sem.at[3])
    for c in (load_feat, load_blk, load_w, load_cot):
        c.start()

    barrier = pltpu.get_barrier_semaphore()
    peers = list(plane_peer.values()) + list(line_peer.values()) + [core_peer]
    for peer in peers:
        pl.semaphore_signal(barrier, inc=1, device_id=peer, device_id_type=MESH)
    pl.semaphore_wait(barrier, len(peers))
    load_feat.wait()

    def slot(j, k):
        return gath.at[j, pl.ds(k * tile, tile)]

    def half(j, k, h):
        return gath.at[j, pl.ds(k * tile + h * (tile // 2), tile // 2)]

    z_copy = {
        d: remote(slot(0, 0), slot(0, Z - d), z_s.at[d], z_r.at[Z - d], line_peer[d])
        for d in (1, 2, 3)
    }
    x_copy = {k: remote(slot(0, k), slot(1, k), x_s.at[k], x_r.at[k], plane_peer[1]) for k in range(Z)}
    y_copy = {k: remote(slot(0, k), slot(2, k), y_s.at[k], y_r.at[k], plane_peer[2]) for k in range(Z)}
    dx_copy = {k: remote(half(2, k, 0), half(3, k, 0), dx_s.at[k], dx_r.at[k], plane_peer[1]) for k in range(Z)}
    dy_copy = {k: remote(half(1, k, 1), half(3, k, 1), dy_s.at[k], dy_r.at[k], plane_peer[2]) for k in range(Z)}

    for d in (1, 3, 2):
        z_copy[d].start()
    x_copy[0].start()
    y_copy[0].start()

    load_blk.wait()

    def build(j):
        for k in range(Z):
            column = (line(k) * PLANE + flip(j)) * 2 + rep
            for p in range(2):
                panel = rep if p == 0 else 1 - rep
                found = jnp.int32(-1)
                for s in range(slots):
                    hit = jnp.logical_and(cols[panel, 0, s] == column, s < counts[panel, 0])
                    found = jnp.where(hit, jnp.int32(s), found)
                block = blk[panel, 0, jnp.maximum(found, 0)]
                keep = (found >= 0).astype(jnp.float32).astype(jnp.bfloat16)
                dense[j, pl.ds(p * tile, tile), pl.ds(k * tile, tile)] = block * keep

    for j in range(2):
        build(j)
    by_arrival = (1, 3, 2)

    def forward(k):
        x_copy[k].wait_recv()
        dy_copy[k].start()
        y_copy[k].wait_recv()
        dx_copy[k].start()

    for k in by_arrival:
        z_copy[Z - k].wait_recv()
        x_copy[k].start()
        y_copy[k].start()
        if k == 1:
            forward(0)
    build(2)
    build(3)
    rows = pl.ds(0, 2 * tile)
    mine, theirs = pl.ds(0, tile), pl.ds(tile, tile)

    def product(j, part):
        return jnp.dot(dense[j, part], gath[j], preferred_element_type=jnp.float32)

    acc_own[...] = product(0, mine)
    acc_oth[...] = product(0, theirs)
    for k in by_arrival:
        forward(k)
    for j in (1, 2):
        acc_own[...] += product(j, mine)
        acc_oth[...] += product(j, theirs)
    for k in (0,) + by_arrival:
        dx_copy[k].wait_recv()
        dy_copy[k].wait_recv()
    acc_oth[...] += product(3, theirs)
    swap = remote(acc_oth, acc_in, p_s.at[0], p_r.at[0], core_peer)
    swap.start()
    acc_own[...] += product(3, mine)
    load_w.wait()
    load_cot.wait()
    swap.wait()

    agg = (acc_own[...] + acc_in[...]).astype(jnp.bfloat16)
    aggs[...] = agg
    pre = jnp.dot(agg, wv[...], preferred_element_type=jnp.float32) + bias[...]
    sig = jax.nn.sigmoid(pre)
    slope = (cotv[...].astype(jnp.float32) * (sig * (1.0 + pre * (1.0 - sig)))).astype(jnp.bfloat16)
    half_rows = width // 2

    def grad_half(which):
        part = aggs[:, pl.ds(pl.multiple_of(which * half_rows, half_rows), half_rows)]
        return lax.dot_general(part, slope, (((0,), (0,)), ((), ())), preferred_element_type=jnp.float32)

    pair_out[...] = grad_half(1 - rep).astype(jnp.bfloat16)
    pair = remote(pair_out, pair_in, p_s.at[1], p_r.at[1], core_peer)
    pair.start()
    total = jnp.sum(slope.astype(jnp.float32), axis=0, keepdims=True)
    lanes = width // 4
    row_id = lax.broadcasted_iota(jnp.int32, (8, lanes), 0)
    spread = jnp.zeros((8, lanes), jnp.float32)
    for i in range(4):
        spread = jnp.where(row_id == i, total[:, i * lanes:(i + 1) * lanes], spread)
    ext[0] = spread
    ext_copy = remote(ext.at[0], ext_pair, p_s.at[2], p_r.at[2], core_peer)
    ext_copy.start()
    half32[...] = grad_half(rep)
    hidv[...] = (pre * sig).astype(jnp.bfloat16)
    store_hid = pltpu.make_async_copy(hidv, hid_out, loc_sem.at[4])
    store_hid.start()

    pair.wait()
    ext_copy.wait()
    both = half32[...] + pair_in[...].astype(jnp.float32)
    half32[...] = both
    half16[...] = both.astype(jnp.bfloat16)
    ext[1] = ext[0] + ext_pair[...]
    quarter = half_rows // PLANE
    rs = []
    for j in (3, 1, 2):
        piece = half16.at[pl.ds(pl.multiple_of(flip(j) * quarter, quarter), quarter)]
        rs.append(remote(piece, plane_in.at[j - 1], rs_s.at[j], rs_r.at[j], plane_peer[j]))
        rs.append(remote(ext.at[1], ext_plane.at[j - 1], rs_s.at[j + 4], rs_r.at[j + 4], plane_peer[j]))
    for c in rs:
        c.start()
    for c in rs:
        c.wait()
    part = half32[pl.ds(pl.multiple_of(q * quarter, quarter), quarter)]
    for j in range(3):
        part = part + plane_in[j].astype(jnp.float32)
    sum32[...] = part
    sum16[...] = part.astype(jnp.bfloat16)
    ext[2] = ext[1] + (ext_plane[0] + ext_plane[1] + ext_plane[2])

    share = quarter // Z
    rs = []
    for d in (2, 1, 3):
        piece = sum16.at[pl.ds(pl.multiple_of(line(d) * share, share), share)]
        rs.append(remote(piece, line_in.at[Z - d - 1], zl_s.at[d], zl_r.at[Z - d], line_peer[d]))
        rs.append(remote(ext.at[2], ext_line.at[Z - d - 1], zl_s.at[d + 4], zl_r.at[Z - d + 4], line_peer[d]))
    for c in rs:
        c.start()
    for c in rs:
        c.wait()
    part = sum32[pl.ds(pl.multiple_of(z * share, share), share)]
    for d in range(3):
        part = part + line_in[d].astype(jnp.float32)

    def region(core, place, height, count):
        start = core * half_rows + place * quarter + height * share
        return fin.at[pl.ds(pl.multiple_of(start, share), count)]

    here = region(rep, q, z, share)
    here[...] = part.astype(jnp.bfloat16)

    zg = [remote(here, here, zg_s.at[d], zg_r.at[Z - d], line_peer[d]) for d in (2, 1, 3)]
    for c in zg:
        c.start()
    everything = ext[2] + (ext_line[0] + ext_line[1] + ext_line[2])
    for i in range(4):
        bias_out[:, i * lanes:(i + 1) * lanes] = everything[i:i + 1]
    for c in zg:
        c.wait()
    mine_q = region(rep, q, 0, quarter)
    pg = {j: remote(mine_q, mine_q, pg_s.at[j], pg_r.at[j], plane_peer[j]) for j in (3, 1, 2)}
    for c in pg.values():
        c.start()
    cg = []
    for j in (0, 1, 2, 3):
        if j:
            pg[j].wait_recv()
        piece = region(rep, flip(j), 0, quarter)
        cg.append(remote(piece, piece, cg_s.at[j], cg_r.at[j], core_peer))
        cg[-1].start()
    for c in cg:
        c.wait()
    store_wg = pltpu.make_async_copy(fin, wg_out, loc_sem.at[5])
    store_wg.start()

    for c in list(z_copy.values()) + list(x_copy.values()) + list(y_copy.values()) + list(dx_copy.values()) + list(dy_copy.values()) + list(pg.values()):
        c.wait_send()
    store_hid.wait()
    store_wg.wait()


def fused_shards(features, col_panels, block_counts, block_values, weight, bias, cotangent):
    tile, width = features.shape
    bf16, f32 = jnp.bfloat16, jnp.float32
    half_rows = width // 2
    quarter = half_rows // PLANE
    share = quarter // Z
    dma = pltpu.SemaphoreType.DMA
    hbm = pl.BlockSpec(memory_space=pl.ANY)
    smem = pl.BlockSpec(memory_space=pltpu.SMEM)
    vmem = pl.BlockSpec(memory_space=pltpu.VMEM)
    hidden, weight_sum, bias_sum = pl.pallas_call(
        fused_kernel,
        out_shape=(
            jax.ShapeDtypeStruct((tile, width), bf16),
            jax.ShapeDtypeStruct((width, width), bf16),
            jax.ShapeDtypeStruct((1, width), f32),
        ),
        in_specs=[hbm, smem, smem, hbm, hbm, vmem, hbm],
        out_specs=(hbm, hbm, vmem),
        scratch_shapes=[
            pltpu.VMEM((PLANE, Z * tile, width), bf16),
            pltpu.VMEM((PLANE, 2 * tile, Z * tile), bf16),
            pltpu.VMEM(block_values.shape, bf16),
            pltpu.VMEM((width, width), bf16),
            pltpu.VMEM((tile, width), bf16),
            pltpu.VMEM((tile, width), f32),
            pltpu.VMEM((tile, width), f32),
            pltpu.VMEM((tile, width), f32),
            pltpu.VMEM((tile, width), bf16),
            pltpu.VMEM((tile, width), bf16),
            pltpu.VMEM((half_rows, width), bf16),
            pltpu.VMEM((half_rows, width), bf16),
            pltpu.VMEM((half_rows, width), f32),
            pltpu.VMEM((half_rows, width), bf16),
            pltpu.VMEM((3, quarter, width), bf16),
            pltpu.VMEM((quarter, width), f32),
            pltpu.VMEM((quarter, width), bf16),
            pltpu.VMEM((3, share, width), bf16),
            pltpu.VMEM((width, width), bf16),
            pltpu.VMEM((3, 8, width // 4), f32),
            pltpu.VMEM((8, width // 4), f32),
            pltpu.VMEM((3, 8, width // 4), f32),
            pltpu.VMEM((3, 8, width // 4), f32),
            dma((6,)),
            dma((4,)), dma((4,)), dma((4,)), dma((4,)), dma((4,)), dma((4,)),
            dma((4,)), dma((4,)), dma((4,)), dma((4,)),
            dma((3,)), dma((3,)),
            dma((8,)), dma((8,)), dma((8,)), dma((8,)),
            dma((4,)), dma((4,)), dma((4,)), dma((4,)), dma((4,)), dma((4,)),
        ],
        compiler_params=pltpu.CompilerParams(
            collective_id=0, has_side_effects=True, vmem_limit_bytes=32 * 1024 * 1024
        ),
        name="fused_layer",
    )(features, col_panels, block_counts, block_values, weight, bias.reshape(1, width), cotangent)
    factor = 1.0 / math.sqrt(lax.axis_size("section") * lax.axis_size("rep") * tile)
    return hidden, weight_sum.astype(f32) * factor, bias_sum[0] * factor


def fits_fused(mesh):
    return dict(mesh.shape) == {"section": Z * PLANE, "rep": 2}


def solution(mesh):
    in_specs = (
        P(("section", "rep"), None),
        P("section", "rep", None),
        P("section", "rep"),
        P("section", "rep", None, None, None),
        P(),
        P(),
        P(("section", "rep"), None),
    )
    out_specs = (P(("section", "rep"), None), P(), P())
    body = fused_shards if fits_fused(mesh) else shards
    return jax.shard_map(body, mesh=mesh, in_specs=in_specs, out_specs=out_specs, check_vma=False)
```

```python
import functools
import math

import jax
import jax.numpy as jnp
from jax import lax
from jax.experimental import pallas as pl
from jax.experimental.pallas import tpu as pltpu
from jax.sharding import PartitionSpec as P


def shards(features, col_panels, block_counts, block_values, weight, bias, cotangent):
    rep_count = lax.axis_size("rep")
    rep_index = lax.axis_index("rep")
    tile_size = block_values.shape[-1]
    feat_width = features.shape[1]
    own_panels = features.shape[0] // tile_size
    row_panels = col_panels.shape[0]
    slot_count = col_panels.shape[2]
    global_cols = col_panels[:, 0, :]
    local_cols = global_cols // (own_panels * rep_count) * own_panels + global_cols % own_panels
    live_counts = block_counts[:, 0]
    slot_mask = jnp.arange(slot_count, dtype=jnp.int32)[None, :] < live_counts[:, None]
    tiles = block_values[:, 0]
    empty = jnp.zeros((row_panels, tile_size, feat_width), jnp.float32)
    gathered = lax.all_gather(features, "section", axis=0, tiled=True)
    all_panels = gathered.reshape(-1, tile_size, feat_width)
    slot_step = 4
    turn_count = (jnp.max(live_counts) + slot_step - 1) // slot_step

    def one_turn(turn, running):
        begin_slot = turn * slot_step
        step_cols = lax.dynamic_slice_in_dim(local_cols, begin_slot, slot_step, 1)
        step_mask = lax.dynamic_slice_in_dim(slot_mask, begin_slot, slot_step, 1)
        step_tiles = lax.dynamic_slice_in_dim(tiles, begin_slot, slot_step, 1)
        step_tiles = jnp.where(step_mask[:, :, None, None], step_tiles, jnp.zeros((), jnp.bfloat16))
        picked = all_panels[step_cols]
        return running + jnp.einsum(
            "gkab,gkbf->gaf", step_tiles, picked, preferred_element_type=jnp.float32
        )

    gathered_sum = lax.fori_loop(0, turn_count, one_turn, empty)
    partial_value = gathered_sum.reshape(row_panels * tile_size, feat_width)
    own_rows = own_panels * tile_size
    summed_all = lax.psum(partial_value, "rep")
    summed_own = lax.dynamic_slice_in_dim(summed_all, rep_index * own_rows, own_rows, 0)
    aggregated = summed_own.astype(jnp.bfloat16)
    pre = jnp.dot(aggregated, weight, preferred_element_type=jnp.float32) + bias
    hidden = jax.nn.silu(pre).astype(jnp.bfloat16)
    sigmoid_pre = jax.nn.sigmoid(pre)
    slope = (
        cotangent.astype(jnp.float32) * (sigmoid_pre * (1.0 + pre * (1.0 - sigmoid_pre)))
    ).astype(jnp.bfloat16)
    local_weight = jnp.einsum("nd,nf->df", aggregated, slope, preferred_element_type=jnp.float32)
    local_bias = jnp.sum(slope.astype(jnp.float32), axis=0)
    weight_sum, bias_sum = lax.psum((local_weight, local_bias), ("section", "rep"))
    node_total = lax.axis_size("section") * rep_count * own_rows
    factor = 1.0 / math.sqrt(node_total)
    return (hidden, weight_sum * factor, bias_sum * factor)

MESH = pl.DeviceIdType.MESH
Z, PLANE = 4, 4


def fused_kernel(
    factor,
    feat, cols, counts, blocks, weight, bias, cot,
    hid_out, wg_out, bias_out,
    gath, dense, blk, wv, cotv, acc_own, acc_oth, acc_in, aggs, hidv,
    pair_out, pair_in, half32, half16, plane_in, sum32, sum16, line_in, fin,
    ext, ext_pair, ext_plane, ext_line,
    loc_sem, z_s, z_r, x_s, x_r, y_s, y_r, dx_s, dx_r, dy_s, dy_r,
    p_s, p_r, rs_s, rs_r, zl_s, zl_r, zg_s, zg_r, pg_s, pg_r, cg_s, cg_r,
):
    tile, width = feat.shape
    me, rep = lax.axis_index("section"), lax.axis_index("rep")
    z, q = me // PLANE, me % PLANE
    y, x = q // 2, q % 2

    def flip(j):
        return (1 - y if j & 2 else y) * 2 + (1 - x if j & 1 else x)

    def line(d):
        return lax.rem(z + d, Z)

    plane_peer = {j: (z * PLANE + flip(j), rep) for j in (1, 2, 3)}
    line_peer = {d: (line(d) * PLANE + q, rep) for d in (1, 2, 3)}
    core_peer = (me, 1 - rep)

    def remote(src, dst, send, recv, peer):
        return pltpu.make_async_remote_copy(
            src_ref=src, dst_ref=dst, send_sem=send, recv_sem=recv,
            device_id=peer, device_id_type=MESH,
        )

    own = gath.at[0, pl.ds(0, tile)]
    load_feat = pltpu.make_async_copy(feat, own, loc_sem.at[0])
    load_blk = pltpu.make_async_copy(blocks, blk, loc_sem.at[1])
    load_w = pltpu.make_async_copy(weight, wv, loc_sem.at[2])
    load_cot = pltpu.make_async_copy(cot, cotv, loc_sem.at[3])
    for c in (load_feat, load_blk, load_w, load_cot):
        c.start()

    barrier = pltpu.get_barrier_semaphore()
    peers = list(plane_peer.values()) + list(line_peer.values()) + [core_peer]
    for peer in peers:
        pl.semaphore_signal(barrier, inc=1, device_id=peer, device_id_type=MESH)
    pl.semaphore_wait(barrier, len(peers))
    load_feat.wait()

    def slot(j, k):
        return gath.at[j, pl.ds(pl.multiple_of(k * tile, tile), tile)]

    def half(j, k, h):
        part = tile // 2
        return gath.at[j, pl.ds(pl.multiple_of(k * tile + h * part, part), part)]

    first = 1 + 2 * (z // 2)
    second = 2 + z - 3 * (z // 2)
    order = (0, first, second, 6 - first - second)
    middle = (z + 1) // 2 == 1

    def pass_on(i, target):
        k = order[i]
        there = lax.rem(z + k - target + Z, Z)
        return remote(slot(0, k), slot(0, there), z_s.at[i], z_r.at[there], (target * PLANE + q, rep))

    up = remote(slot(0, 0), slot(0, Z - 1), z_s.at[0], z_r.at[Z - 1], ((z + 1) * PLANE + q, rep))
    down = remote(slot(0, 0), slot(0, 1), z_s.at[4], z_r.at[1], ((z - 1) * PLANE + q, rep))
    relay = {1: pass_on(1, lax.rem(3 * z + 1, Z)), 2: pass_on(2, Z - 1 - z), 3: pass_on(3, lax.rem(3 * z + 1, Z))}

    @pl.when(z < Z - 1)
    def _():
        up.start()

    @pl.when(z > 0)
    def _():
        down.start()

    x_copy = [remote(slot(0, k), slot(1, k), x_s.at[k], x_r.at[k], plane_peer[1]) for k in order]
    y_copy = [remote(slot(0, k), slot(2, k), y_s.at[k], y_r.at[k], plane_peer[2]) for k in order]
    dx_copy = [remote(half(2, k, 0), half(3, k, 0), dx_s.at[k], dx_r.at[k], plane_peer[1]) for k in order]
    dy_copy = [remote(half(1, k, 1), half(3, k, 1), dy_s.at[k], dy_r.at[k], plane_peer[2]) for k in order]
    x_copy[0].start()
    y_copy[0].start()

    def live(p):
        panel = rep if p == 0 else 1 - rep
        count = counts[panel]
        return [jnp.where(s < count, cols[panel, 0, s], -1) for s in range(cols.shape[2])]

    lists = [live(0), live(1)]
    load_blk.wait()
    for j in range(PLANE):
        for k in range(Z):
            for p in range(2):
                panel = rep if p == 0 else 1 - rep
                column = (line(k) * PLANE + flip(j)) * 2 + rep
                place = jnp.int32(0)
                for s, listed in enumerate(lists[p]):
                    place = jnp.where(listed == column, jnp.int32(s + 1), place)
                block = blk[panel, 0, jnp.maximum(place - 1, 0)]
                keep = jnp.minimum(place, 1).astype(jnp.float32).astype(jnp.bfloat16)
                dense[j, pl.ds(p * tile, tile), pl.ds(k * tile, tile)] = block * keep

    def forward(i):
        x_copy[i].wait_recv()
        dy_copy[i].start()
        y_copy[i].wait_recv()
        dx_copy[i].start()

    for i in (1, 2, 3):
        pltpu.make_async_copy(slot(0, 0), slot(0, order[i]), z_r.at[order[i]]).wait()

        @pl.when(middle)
        def _():
            relay[i].start()

        x_copy[i].start()
        y_copy[i].start()
        if i < 3:
            forward(i - 1)
    mine, theirs = pl.ds(0, tile), pl.ds(tile, tile)

    def product(j, part):
        return jnp.dot(dense[j, part], gath[j], preferred_element_type=jnp.float32)

    acc_own[...] = product(0, mine)
    acc_oth[...] = product(0, theirs)
    forward(2)
    forward(3)
    for j in (1, 2):
        acc_own[...] += product(j, mine)
        acc_oth[...] += product(j, theirs)
    for i in range(Z):
        dx_copy[i].wait_recv()
        dy_copy[i].wait_recv()
    acc_oth[...] += product(3, theirs)
    swap = remote(acc_oth, acc_in, p_s.at[0], p_r.at[0], core_peer)
    swap.start()
    acc_own[...] += product(3, mine)
    load_w.wait()
    load_cot.wait()
    swap.wait()

    agg = (acc_own[...] + acc_in[...]).astype(jnp.bfloat16)
    aggs[...] = agg
    pre = jnp.dot(agg, wv[...], preferred_element_type=jnp.float32) + bias[...]
    sig = jax.nn.sigmoid(pre)
    slope = (cotv[...].astype(jnp.float32) * (sig * (1.0 + pre * (1.0 - sig)))).astype(jnp.bfloat16)
    half_rows = width // 2

    def grad_half(which):
        part = aggs[:, pl.ds(pl.multiple_of(which * half_rows, half_rows), half_rows)]
        return lax.dot_general(part, slope, (((0,), (0,)), ((), ())), preferred_element_type=jnp.float32)

    pair_out[...] = grad_half(1 - rep).astype(jnp.bfloat16)
    pair = remote(pair_out, pair_in, p_s.at[1], p_r.at[1], core_peer)
    pair.start()
    total = jnp.sum(slope.astype(jnp.float32), axis=0, keepdims=True)
    lanes = width // 4
    row_id = lax.broadcasted_iota(jnp.int32, (8, lanes), 0)
    spread = jnp.zeros((8, lanes), jnp.float32)
    for i in range(4):
        spread = jnp.where(row_id == i, total[:, i * lanes:(i + 1) * lanes], spread)
    ext[0] = spread
    ext_copy = remote(ext.at[0], ext_pair, p_s.at[2], p_r.at[2], core_peer)
    ext_copy.start()
    half32[...] = grad_half(rep)
    hidv[...] = (pre * sig).astype(jnp.bfloat16)
    store_hid = pltpu.make_async_copy(hidv, hid_out, loc_sem.at[4])
    store_hid.start()

    pair.wait()
    ext_copy.wait()
    both = half32[...] + pair_in[...].astype(jnp.float32)
    half32[...] = both
    half16[...] = both.astype(jnp.bfloat16)
    ext[1] = ext[0] + ext_pair[...]
    quarter = half_rows // PLANE
    rs = []
    for j in (3, 1, 2):
        piece = half16.at[pl.ds(pl.multiple_of(flip(j) * quarter, quarter), quarter)]
        rs.append(remote(piece, plane_in.at[j - 1], rs_s.at[j], rs_r.at[j], plane_peer[j]))
        rs.append(remote(ext.at[1], ext_plane.at[j - 1], rs_s.at[j + 4], rs_r.at[j + 4], plane_peer[j]))
    for c in rs:
        c.start()
    for c in rs:
        c.wait()
    part = half32[pl.ds(pl.multiple_of(q * quarter, quarter), quarter)]
    for j in range(3):
        part = part + plane_in[j].astype(jnp.float32)
    sum32[...] = part
    sum16[...] = part.astype(jnp.bfloat16)
    ext[2] = ext[1] + (ext_plane[0] + ext_plane[1] + ext_plane[2])

    share = quarter // Z
    rs = []
    for d in (2, 1, 3):
        piece = sum16.at[pl.ds(pl.multiple_of(line(d) * share, share), share)]
        rs.append(remote(piece, line_in.at[Z - d - 1], zl_s.at[d], zl_r.at[Z - d], line_peer[d]))
        rs.append(remote(ext.at[2], ext_line.at[Z - d - 1], zl_s.at[d + 4], zl_r.at[Z - d + 4], line_peer[d]))
    for c in rs:
        c.start()
    for c in rs:
        c.wait()
    part = sum32[pl.ds(pl.multiple_of(z * share, share), share)]
    for d in range(3):
        part = part + line_in[d].astype(jnp.float32)

    def region(core, place, height, count):
        start = core * half_rows + place * quarter + height * share
        return fin.at[pl.ds(pl.multiple_of(start, share), count)]

    here = region(rep, q, z, share)
    here[...] = part.astype(jnp.bfloat16)

    zg = [remote(here, here, zg_s.at[d], zg_r.at[Z - d], line_peer[d]) for d in (2, 1, 3)]
    for c in zg:
        c.start()
    everything = ext[2] + (ext_line[0] + ext_line[1] + ext_line[2])
    for i in range(4):
        bias_out[:, i * lanes:(i + 1) * lanes] = everything[i:i + 1] * factor
    for c in zg:
        c.wait()
    mine_q = region(rep, q, 0, quarter)
    pg = {j: remote(mine_q, mine_q, pg_s.at[j], pg_r.at[j], plane_peer[j]) for j in (3, 1, 2)}
    for c in pg.values():
        c.start()
    cg = []
    for j in (0, 1, 2, 3):
        if j:
            pg[j].wait_recv()
        piece = region(rep, flip(j), 0, quarter)
        cg.append(remote(piece, piece, cg_s.at[j], cg_r.at[j], core_peer))
        cg[-1].start()
    for c in cg:
        c.wait()
    store_wg = pltpu.make_async_copy(fin, wg_out, loc_sem.at[5])
    store_wg.start()

    for c in x_copy + y_copy + dx_copy + dy_copy + list(pg.values()):
        c.wait_send()

    @pl.when(z < Z - 1)
    def _():
        up.wait_send()

    @pl.when(z > 0)
    def _():
        down.wait_send()

    @pl.when(middle)
    def _():
        for c in relay.values():
            c.wait_send()

    store_hid.wait()
    store_wg.wait()


def fused_shards(features, col_panels, block_counts, block_values, weight, bias, cotangent):
    tile, width = features.shape
    bf16, f32 = jnp.bfloat16, jnp.float32
    half_rows = width // 2
    quarter = half_rows // PLANE
    share = quarter // Z
    dma = pltpu.SemaphoreType.DMA
    hbm = pl.BlockSpec(memory_space=pl.ANY)
    smem = pl.BlockSpec(memory_space=pltpu.SMEM)
    vmem = pl.BlockSpec(memory_space=pltpu.VMEM)
    factor = 1.0 / math.sqrt(lax.axis_size("section") * lax.axis_size("rep") * tile)
    hidden, weight_sum, bias_sum = pl.pallas_call(
        functools.partial(fused_kernel, factor),
        out_shape=(
            jax.ShapeDtypeStruct((tile, width), bf16),
            jax.ShapeDtypeStruct((width, width), bf16),
            jax.ShapeDtypeStruct((1, width), f32),
        ),
        in_specs=[hbm, smem, smem, hbm, hbm, vmem, hbm],
        out_specs=(hbm, hbm, vmem),
        scratch_shapes=[
            pltpu.VMEM((PLANE, Z * tile, width), bf16),
            pltpu.VMEM((PLANE, 2 * tile, Z * tile), bf16),
            pltpu.VMEM(block_values.shape, bf16),
            pltpu.VMEM((width, width), bf16),
            pltpu.VMEM((tile, width), bf16),
            pltpu.VMEM((tile, width), f32),
            pltpu.VMEM((tile, width), f32),
            pltpu.VMEM((tile, width), f32),
            pltpu.VMEM((tile, width), bf16),
            pltpu.VMEM((tile, width), bf16),
            pltpu.VMEM((half_rows, width), bf16),
            pltpu.VMEM((half_rows, width), bf16),
            pltpu.VMEM((half_rows, width), f32),
            pltpu.VMEM((half_rows, width), bf16),
            pltpu.VMEM((3, quarter, width), bf16),
            pltpu.VMEM((quarter, width), f32),
            pltpu.VMEM((quarter, width), bf16),
            pltpu.VMEM((3, share, width), bf16),
            pltpu.VMEM((width, width), bf16),
            pltpu.VMEM((3, 8, width // 4), f32),
            pltpu.VMEM((8, width // 4), f32),
            pltpu.VMEM((3, 8, width // 4), f32),
            pltpu.VMEM((3, 8, width // 4), f32),
            dma((6,)),
            dma((5,)), dma((4,)), dma((4,)), dma((4,)), dma((4,)), dma((4,)),
            dma((4,)), dma((4,)), dma((4,)), dma((4,)),
            dma((3,)), dma((3,)),
            dma((8,)), dma((8,)), dma((8,)), dma((8,)),
            dma((4,)), dma((4,)), dma((4,)), dma((4,)), dma((4,)), dma((4,)),
        ],
        compiler_params=pltpu.CompilerParams(
            collective_id=0, has_side_effects=True, vmem_limit_bytes=60 * 1024 * 1024
        ),
        name="fused_layer",
    )(features, col_panels, block_counts.reshape(-1), block_values, weight, bias.reshape(1, width), cotangent)
    return hidden, weight_sum.astype(f32) * factor, bias_sum[0]


def fits_fused(mesh):
    return dict(mesh.shape) == {"section": Z * PLANE, "rep": 2}


def solution(mesh):
    in_specs = (
        P(("section", "rep"), None),
        P("section", "rep", None),
        P("section", "rep"),
        P("section", "rep", None, None, None),
        P(),
        P(),
        P(("section", "rep"), None),
    )
    out_specs = (P(("section", "rep"), None), P(), P())
    body = fused_shards if fits_fused(mesh) else shards
    return jax.shard_map(body, mesh=mesh, in_specs=in_specs, out_specs=out_specs, check_vma=False)
```

```python
import functools
import math

import jax
import jax.numpy as jnp
from jax import lax
from jax.experimental import pallas as pl
from jax.experimental.pallas import tpu as pltpu
from jax.sharding import PartitionSpec as P


def shards(features, col_panels, block_counts, block_values, weight, bias, cotangent):
    rep_count = lax.axis_size("rep")
    rep_index = lax.axis_index("rep")
    tile_size = block_values.shape[-1]
    feat_width = features.shape[1]
    own_panels = features.shape[0] // tile_size
    row_panels = col_panels.shape[0]
    slot_count = col_panels.shape[2]
    global_cols = col_panels[:, 0, :]
    local_cols = global_cols // (own_panels * rep_count) * own_panels + global_cols % own_panels
    live_counts = block_counts[:, 0]
    slot_mask = jnp.arange(slot_count, dtype=jnp.int32)[None, :] < live_counts[:, None]
    tiles = block_values[:, 0]
    empty = jnp.zeros((row_panels, tile_size, feat_width), jnp.float32)
    gathered = lax.all_gather(features, "section", axis=0, tiled=True)
    all_panels = gathered.reshape(-1, tile_size, feat_width)
    slot_step = 4
    turn_count = (jnp.max(live_counts) + slot_step - 1) // slot_step

    def one_turn(turn, running):
        begin_slot = turn * slot_step
        step_cols = lax.dynamic_slice_in_dim(local_cols, begin_slot, slot_step, 1)
        step_mask = lax.dynamic_slice_in_dim(slot_mask, begin_slot, slot_step, 1)
        step_tiles = lax.dynamic_slice_in_dim(tiles, begin_slot, slot_step, 1)
        step_tiles = jnp.where(step_mask[:, :, None, None], step_tiles, jnp.zeros((), jnp.bfloat16))
        picked = all_panels[step_cols]
        return running + jnp.einsum(
            "gkab,gkbf->gaf", step_tiles, picked, preferred_element_type=jnp.float32
        )

    gathered_sum = lax.fori_loop(0, turn_count, one_turn, empty)
    partial_value = gathered_sum.reshape(row_panels * tile_size, feat_width)
    own_rows = own_panels * tile_size
    summed_all = lax.psum(partial_value, "rep")
    summed_own = lax.dynamic_slice_in_dim(summed_all, rep_index * own_rows, own_rows, 0)
    aggregated = summed_own.astype(jnp.bfloat16)
    pre = jnp.dot(aggregated, weight, preferred_element_type=jnp.float32) + bias
    hidden = jax.nn.silu(pre).astype(jnp.bfloat16)
    sigmoid_pre = jax.nn.sigmoid(pre)
    slope = (
        cotangent.astype(jnp.float32) * (sigmoid_pre * (1.0 + pre * (1.0 - sigmoid_pre)))
    ).astype(jnp.bfloat16)
    local_weight = jnp.einsum("nd,nf->df", aggregated, slope, preferred_element_type=jnp.float32)
    local_bias = jnp.sum(slope.astype(jnp.float32), axis=0)
    weight_sum, bias_sum = lax.psum((local_weight, local_bias), ("section", "rep"))
    node_total = lax.axis_size("section") * rep_count * own_rows
    factor = 1.0 / math.sqrt(node_total)
    return (hidden, weight_sum * factor, bias_sum * factor)

MESH = pl.DeviceIdType.MESH
Z, PLANE = 4, 4
CHUNKS = 2


def fused_kernel(
    factor,
    feat, cols, counts, blocks, weight, bias, cot,
    hid_out, wg_out, bias_out,
    gath, dense, blk, wv, cotv, acc_own, acc_oth, acc_in, aggs, hidv,
    pair_out, pair_in, half32, half16, plane_in, sum32, sum16, line_in, fin,
    ext, ext_pair, ext_plane, ext_line,
    loc_sem, z_s, z_r, x_s, x_r, y_s, y_r, dx_s, dx_r, dy_s, dy_r,
    p_s, p_r, e_s, e_r, rs_s, rs_r, zl_s, zl_r, zg_s, zg_r, pg_s, pg_r, cg_s, cg_r,
):
    tile, width = feat.shape
    me, rep = lax.axis_index("section"), lax.axis_index("rep")
    z, q = me // PLANE, me % PLANE
    y, x = q // 2, q % 2

    def flip(j):
        return (1 - y if j & 2 else y) * 2 + (1 - x if j & 1 else x)

    def line(d):
        return lax.rem(z + d, Z)

    plane_peer = {j: (z * PLANE + flip(j), rep) for j in (1, 2, 3)}
    line_peer = {d: (line(d) * PLANE + q, rep) for d in (1, 2, 3)}
    core_peer = (me, 1 - rep)

    def remote(src, dst, send, recv, peer):
        return pltpu.make_async_remote_copy(
            src_ref=src, dst_ref=dst, send_sem=send, recv_sem=recv,
            device_id=peer, device_id_type=MESH,
        )

    own = gath.at[0, pl.ds(0, tile)]
    load_feat = pltpu.make_async_copy(feat, own, loc_sem.at[0])
    load_blk = pltpu.make_async_copy(blocks, blk, loc_sem.at[1])
    load_w = pltpu.make_async_copy(weight, wv, loc_sem.at[2])
    load_cot = pltpu.make_async_copy(cot, cotv, loc_sem.at[3])
    for c in (load_feat, load_blk, load_w, load_cot):
        c.start()

    barrier = pltpu.get_barrier_semaphore()
    peers = list(plane_peer.values()) + list(line_peer.values()) + [core_peer]
    for peer in peers:
        pl.semaphore_signal(barrier, inc=1, device_id=peer, device_id_type=MESH)
    pl.semaphore_wait(barrier, len(peers))
    load_feat.wait()

    def slot(j, k):
        return gath.at[j, pl.ds(pl.multiple_of(k * tile, tile), tile)]

    def half(j, k, h):
        part = tile // 2
        return gath.at[j, pl.ds(pl.multiple_of(k * tile + h * part, part), part)]

    first = 1 + 2 * (z // 2)
    second = 2 + z - 3 * (z // 2)
    order = (0, first, second, 6 - first - second)
    middle = (z + 1) // 2 == 1

    def pass_on(i, target):
        k = order[i]
        there = lax.rem(z + k - target + Z, Z)
        return remote(slot(0, k), slot(0, there), z_s.at[i], z_r.at[there], (target * PLANE + q, rep))

    up = remote(slot(0, 0), slot(0, Z - 1), z_s.at[0], z_r.at[Z - 1], ((z + 1) * PLANE + q, rep))
    down = remote(slot(0, 0), slot(0, 1), z_s.at[4], z_r.at[1], ((z - 1) * PLANE + q, rep))
    relay = {1: pass_on(1, lax.rem(3 * z + 1, Z)), 2: pass_on(2, Z - 1 - z), 3: pass_on(3, lax.rem(3 * z + 1, Z))}

    @pl.when(z < Z - 1)
    def _():
        up.start()

    @pl.when(z > 0)
    def _():
        down.start()

    x_copy = [remote(slot(0, k), slot(1, k), x_s.at[k], x_r.at[k], plane_peer[1]) for k in order]
    y_copy = [remote(slot(0, k), slot(2, k), y_s.at[k], y_r.at[k], plane_peer[2]) for k in order]
    dx_copy = [remote(half(2, k, 0), half(3, k, 0), dx_s.at[k], dx_r.at[k], plane_peer[1]) for k in order]
    dy_copy = [remote(half(1, k, 1), half(3, k, 1), dy_s.at[k], dy_r.at[k], plane_peer[2]) for k in order]
    x_copy[0].start()
    y_copy[0].start()

    def live(p):
        panel = rep if p == 0 else 1 - rep
        count = counts[panel]
        return [jnp.where(s < count, cols[panel, 0, s], -1) for s in range(cols.shape[2])]

    lists = [live(0), live(1)]
    load_blk.wait()
    for j in range(PLANE):
        for k in range(Z):
            for p in range(2):
                panel = rep if p == 0 else 1 - rep
                column = (line(k) * PLANE + flip(j)) * 2 + rep
                place = jnp.int32(0)
                for s, listed in enumerate(lists[p]):
                    place = jnp.where(listed == column, jnp.int32(s + 1), place)
                block = blk[panel, 0, jnp.maximum(place - 1, 0)]
                keep = jnp.minimum(place, 1).astype(jnp.float32).astype(jnp.bfloat16)
                dense[j, pl.ds(p * tile, tile), pl.ds(k * tile, tile)] = block * keep

    def forward(i):
        x_copy[i].wait_recv()
        dy_copy[i].start()
        y_copy[i].wait_recv()
        dx_copy[i].start()

    for i in (1, 2, 3):
        pltpu.make_async_copy(slot(0, 0), slot(0, order[i]), z_r.at[order[i]]).wait()

        @pl.when(middle)
        def _():
            relay[i].start()

        x_copy[i].start()
        y_copy[i].start()
        if i < 3:
            forward(i - 1)
    mine, theirs = pl.ds(0, tile), pl.ds(tile, tile)

    def product(j, part):
        return jnp.dot(dense[j, part], gath[j], preferred_element_type=jnp.float32)

    acc_own[...] = product(0, mine)
    acc_oth[...] = product(0, theirs)
    forward(2)
    forward(3)
    for j in (1, 2):
        acc_own[...] += product(j, mine)
        acc_oth[...] += product(j, theirs)
    for i in range(Z):
        dx_copy[i].wait_recv()
        dy_copy[i].wait_recv()
    acc_oth[...] += product(3, theirs)
    swap = remote(acc_oth, acc_in, p_s.at[0], p_r.at[0], core_peer)
    swap.start()
    acc_own[...] += product(3, mine)
    load_w.wait()
    load_cot.wait()
    swap.wait()

    agg = (acc_own[...] + acc_in[...]).astype(jnp.bfloat16)
    aggs[...] = agg
    pre = jnp.dot(agg, wv[...], preferred_element_type=jnp.float32) + bias[...]
    sig = jax.nn.sigmoid(pre)
    slope = (cotv[...].astype(jnp.float32) * (sig * (1.0 + pre * (1.0 - sig)))).astype(jnp.bfloat16)
    half_rows, columns = width // 2, width // CHUNKS
    quarter = half_rows // PLANE
    share = quarter // Z
    aligned = pl.multiple_of

    def grad_half(which, c):
        part = aggs[:, pl.ds(aligned(which * half_rows, half_rows), half_rows)]
        cut = slope[:, c * columns:(c + 1) * columns]
        return lax.dot_general(part, cut, (((0,), (0,)), ((), ())), preferred_element_type=jnp.float32)

    chunks = range(CHUNKS)
    pair = [remote(pair_out.at[c], pair_in.at[c], p_s.at[c + 2], p_r.at[c + 2], core_peer) for c in chunks]
    for c in chunks:
        pair_out[c] = grad_half(1 - rep, c).astype(jnp.bfloat16)
        pair[c].start()
    total = jnp.sum(slope.astype(jnp.float32), axis=0, keepdims=True)
    lanes = width // 4
    row_id = lax.broadcasted_iota(jnp.int32, (8, lanes), 0)
    spread = jnp.zeros((8, lanes), jnp.float32)
    for i in range(4):
        spread = jnp.where(row_id == i, total[:, i * lanes:(i + 1) * lanes], spread)
    ext[0] = spread
    ext_copy = remote(ext.at[0], ext_pair, p_s.at[1], p_r.at[1], core_peer)
    ext_copy.start()

    plane_sum = []
    for c in chunks:
        own_half = grad_half(rep, c)
        pair[c].wait_recv()
        both = own_half + pair_in[c].astype(jnp.float32)
        half32[c] = both
        half16[c] = both.astype(jnp.bfloat16)
        copies = []
        for j in (3, 1, 2):
            piece = half16.at[c, pl.ds(aligned(flip(j) * quarter, quarter), quarter)]
            copies.append(remote(piece, plane_in.at[c, j - 1], rs_s.at[c, j], rs_r.at[c, j], plane_peer[j]))
        for copy in copies:
            copy.start()
        plane_sum.append(copies)
    ext_copy.wait()
    ext[1] = ext[0] + ext_pair[...]
    ext_sum = [remote(ext.at[1], ext_plane.at[j - 1], e_s.at[j], e_r.at[j], plane_peer[j]) for j in (1, 2, 3)]
    for copy in ext_sum:
        copy.start()
    hidv[...] = (pre * sig).astype(jnp.bfloat16)
    store_hid = pltpu.make_async_copy(hidv, hid_out, loc_sem.at[4])
    store_hid.start()

    line_sum = []
    for c in chunks:
        for copy in plane_sum[c]:
            copy.wait_recv()
        part = half32[c, pl.ds(aligned(q * quarter, quarter), quarter)]
        for j in range(3):
            part = part + plane_in[c, j].astype(jnp.float32)
        sum32[c] = part
        sum16[c] = part.astype(jnp.bfloat16)
        copies = []
        for d in (2, 1, 3):
            piece = sum16.at[c, pl.ds(aligned(line(d) * share, share), share)]
            copies.append(remote(piece, line_in.at[c, Z - d - 1], zl_s.at[c, d], zl_r.at[c, Z - d], line_peer[d]))
        for copy in copies:
            copy.start()
        line_sum.append(copies)
    for copy in ext_sum:
        copy.wait()
    ext[2] = ext[1] + (ext_plane[0] + ext_plane[1] + ext_plane[2])
    ext_line_sum = [remote(ext.at[2], ext_line.at[Z - d - 1], e_s.at[d + 4], e_r.at[Z - d + 4], line_peer[d]) for d in (1, 2, 3)]
    for copy in ext_line_sum:
        copy.start()

    def region(c, core, place, height, count):
        start = core * half_rows + place * quarter + height * share
        return fin.at[c, pl.ds(aligned(start, share), count)]

    line_all = []
    for c in chunks:
        for copy in line_sum[c]:
            copy.wait_recv()
        part = sum32[c, pl.ds(aligned(z * share, share), share)]
        for d in range(3):
            part = part + line_in[c, d].astype(jnp.float32)
        here = region(c, rep, q, z, share)
        here[...] = part.astype(jnp.bfloat16)
        copies = [remote(here, here, zg_s.at[c, d], zg_r.at[c, Z - d], line_peer[d]) for d in (2, 1, 3)]
        for copy in copies:
            copy.start()
        line_all.append(copies)
    for copy in ext_line_sum:
        copy.wait()
    everything = ext[2] + (ext_line[0] + ext_line[1] + ext_line[2])
    for i in range(4):
        bias_out[:, i * lanes:(i + 1) * lanes] = everything[i:i + 1] * factor
    plane_all, core_all = [], []
    for c in chunks:
        for copy in line_all[c]:
            copy.wait_recv()
        own_q = region(c, rep, q, 0, quarter)
        copies = {j: remote(own_q, own_q, pg_s.at[c, j], pg_r.at[c, j], plane_peer[j]) for j in (3, 1, 2)}
        for copy in copies.values():
            copy.start()
        plane_all.append(copies)
        core_all.append(remote(own_q, own_q, cg_s.at[c, 0], cg_r.at[c, 0], core_peer))
        core_all[-1].start()
    for c in chunks:
        for j in (1, 2, 3):
            plane_all[c][j].wait_recv()
            piece = region(c, rep, flip(j), 0, quarter)
            core_all.append(remote(piece, piece, cg_s.at[c, j], cg_r.at[c, j], core_peer))
            core_all[-1].start()
    for copy in core_all:
        copy.wait()
    store_wg = []
    for c in chunks:
        store_wg.append(pltpu.make_async_copy(fin.at[c], wg_out.at[:, pl.ds(c * columns, columns)], loc_sem.at[5 + c]))
        store_wg[-1].start()
    for copies in plane_sum + line_sum + line_all + [list(p.values()) for p in plane_all] + [pair]:
        for copy in copies:
            copy.wait_send()

    for c in x_copy + y_copy + dx_copy + dy_copy:
        c.wait_send()

    @pl.when(z < Z - 1)
    def _():
        up.wait_send()

    @pl.when(z > 0)
    def _():
        down.wait_send()

    @pl.when(middle)
    def _():
        for c in relay.values():
            c.wait_send()

    store_hid.wait()
    for copy in store_wg:
        copy.wait()


def fused_shards(features, col_panels, block_counts, block_values, weight, bias, cotangent):
    tile, width = features.shape
    bf16, f32 = jnp.bfloat16, jnp.float32
    half_rows, columns = width // 2, width // CHUNKS
    quarter = half_rows // PLANE
    share = quarter // Z
    dma = pltpu.SemaphoreType.DMA
    hbm = pl.BlockSpec(memory_space=pl.ANY)

    smem = pl.BlockSpec(memory_space=pltpu.SMEM)
    vmem = pl.BlockSpec(memory_space=pltpu.VMEM)
    factor = 1.0 / math.sqrt(lax.axis_size("section") * lax.axis_size("rep") * tile)
    hidden, weight_sum, bias_sum = pl.pallas_call(
        functools.partial(fused_kernel, factor),
        out_shape=(
            jax.ShapeDtypeStruct((tile, width), bf16),
            jax.ShapeDtypeStruct((width, width), bf16),
            jax.ShapeDtypeStruct((1, width), f32),
        ),
        in_specs=[hbm, smem, smem, hbm, hbm, vmem, hbm],
        out_specs=(hbm, hbm, vmem),
        scratch_shapes=[
            pltpu.VMEM((PLANE, Z * tile, width), bf16),
            pltpu.VMEM((PLANE, 2 * tile, Z * tile), bf16),
            pltpu.VMEM(block_values.shape, bf16),
            pltpu.VMEM((width, width), bf16),
            pltpu.VMEM((tile, width), bf16),
            pltpu.VMEM((tile, width), f32),
            pltpu.VMEM((tile, width), f32),
            pltpu.VMEM((tile, width), f32),
            pltpu.VMEM((tile, width), bf16),
            pltpu.VMEM((tile, width), bf16),
            pltpu.VMEM((CHUNKS, half_rows, columns), bf16),
            pltpu.VMEM((CHUNKS, half_rows, columns), bf16),
            pltpu.VMEM((CHUNKS, half_rows, columns), f32),
            pltpu.VMEM((CHUNKS, half_rows, columns), bf16),
            pltpu.VMEM((CHUNKS, 3, quarter, columns), bf16),
            pltpu.VMEM((CHUNKS, quarter, columns), f32),
            pltpu.VMEM((CHUNKS, quarter, columns), bf16),
            pltpu.VMEM((CHUNKS, 3, share, columns), bf16),
            pltpu.VMEM((CHUNKS, width, columns), bf16),
            pltpu.VMEM((3, 8, width // 4), f32),
            pltpu.VMEM((8, width // 4), f32),
            pltpu.VMEM((3, 8, width // 4), f32),
            pltpu.VMEM((3, 8, width // 4), f32),
            dma((5 + CHUNKS,)),
            dma((5,)), dma((4,)), dma((4,)), dma((4,)), dma((4,)), dma((4,)),
            dma((4,)), dma((4,)), dma((4,)), dma((4,)),
            dma((2 + CHUNKS,)), dma((2 + CHUNKS,)), dma((8,)), dma((8,)),
        ] + [dma((CHUNKS, 4))] * 10,
        compiler_params=pltpu.CompilerParams(
            collective_id=0, has_side_effects=True, vmem_limit_bytes=60 * 1024 * 1024
        ),
        name="fused_layer",
    )(features, col_panels, block_counts.reshape(-1), block_values, weight, bias.reshape(1, width), cotangent)
    return hidden, weight_sum.astype(f32) * factor, bias_sum[0]


def fits_fused(mesh):
    return dict(mesh.shape) == {"section": Z * PLANE, "rep": 2}


def solution(mesh):
    in_specs = (
        P(("section", "rep"), None),
        P("section", "rep", None),
        P("section", "rep"),
        P("section", "rep", None, None, None),
        P(),
        P(),
        P(("section", "rep"), None),
    )
    out_specs = (P(("section", "rep"), None), P(), P())
    body = fused_shards if fits_fused(mesh) else shards
    return jax.shard_map(body, mesh=mesh, in_specs=in_specs, out_specs=out_specs, check_vma=False)
```

```python
import functools
import math

import jax
import jax.numpy as jnp
from jax import lax
from jax.experimental import pallas as pl
from jax.experimental.pallas import tpu as pltpu
from jax.sharding import PartitionSpec as P


def shards(features, col_panels, block_counts, block_values, weight, bias, cotangent):
    rep_count = lax.axis_size("rep")
    rep_index = lax.axis_index("rep")
    tile_size = block_values.shape[-1]
    feat_width = features.shape[1]
    own_panels = features.shape[0] // tile_size
    row_panels = col_panels.shape[0]
    slot_count = col_panels.shape[2]
    global_cols = col_panels[:, 0, :]
    local_cols = global_cols // (own_panels * rep_count) * own_panels + global_cols % own_panels
    live_counts = block_counts[:, 0]
    slot_mask = jnp.arange(slot_count, dtype=jnp.int32)[None, :] < live_counts[:, None]
    tiles = block_values[:, 0]
    empty = jnp.zeros((row_panels, tile_size, feat_width), jnp.float32)
    gathered = lax.all_gather(features, "section", axis=0, tiled=True)
    all_panels = gathered.reshape(-1, tile_size, feat_width)
    slot_step = 4
    turn_count = (jnp.max(live_counts) + slot_step - 1) // slot_step

    def one_turn(turn, running):
        begin_slot = turn * slot_step
        step_cols = lax.dynamic_slice_in_dim(local_cols, begin_slot, slot_step, 1)
        step_mask = lax.dynamic_slice_in_dim(slot_mask, begin_slot, slot_step, 1)
        step_tiles = lax.dynamic_slice_in_dim(tiles, begin_slot, slot_step, 1)
        step_tiles = jnp.where(step_mask[:, :, None, None], step_tiles, jnp.zeros((), jnp.bfloat16))
        picked = all_panels[step_cols]
        return running + jnp.einsum(
            "gkab,gkbf->gaf", step_tiles, picked, preferred_element_type=jnp.float32
        )

    gathered_sum = lax.fori_loop(0, turn_count, one_turn, empty)
    partial_value = gathered_sum.reshape(row_panels * tile_size, feat_width)
    own_rows = own_panels * tile_size
    summed_all = lax.psum(partial_value, "rep")
    summed_own = lax.dynamic_slice_in_dim(summed_all, rep_index * own_rows, own_rows, 0)
    aggregated = summed_own.astype(jnp.bfloat16)
    pre = jnp.dot(aggregated, weight, preferred_element_type=jnp.float32) + bias
    hidden = jax.nn.silu(pre).astype(jnp.bfloat16)
    sigmoid_pre = jax.nn.sigmoid(pre)
    slope = (
        cotangent.astype(jnp.float32) * (sigmoid_pre * (1.0 + pre * (1.0 - sigmoid_pre)))
    ).astype(jnp.bfloat16)
    local_weight = jnp.einsum("nd,nf->df", aggregated, slope, preferred_element_type=jnp.float32)
    local_bias = jnp.sum(slope.astype(jnp.float32), axis=0)
    weight_sum, bias_sum = lax.psum((local_weight, local_bias), ("section", "rep"))
    node_total = lax.axis_size("section") * rep_count * own_rows
    factor = 1.0 / math.sqrt(node_total)
    return (hidden, weight_sum * factor, bias_sum * factor)

MESH = pl.DeviceIdType.MESH
Z, PLANE = 4, 4
CHUNKS = 2
PARTS = 4


def fused_kernel(
    factor,
    feat, cols, counts, blocks, weight, bias, cot,
    hid_out, wg_out, bias_out,
    gath, dense, blk, wv, cotv, acc_own, acc_oth, acc_in, aggs, hidv,
    pair_out, pair_in, half32, half16, plane_in, sum32, sum16, line_in, fin,
    ext, ext_pair, ext_plane, ext_line,
    loc_sem, z_s, z_r, x_s, x_r, y_s, y_r, dx_s, dx_r, dy_s, dy_r,
    p_s, p_r, e_s, e_r, rs_s, rs_r, zl_s, zl_r, pg_s, pg_r, cg_s, cg_r,
):
    tile, width = feat.shape
    me, rep = lax.axis_index("section"), lax.axis_index("rep")
    z, q = me // PLANE, me % PLANE
    y, x = q // 2, q % 2

    def flip(j):
        return (1 - y if j & 2 else y) * 2 + (1 - x if j & 1 else x)

    def line(d):
        return lax.rem(z + d, Z)

    plane_peer = {j: (z * PLANE + flip(j), rep) for j in (1, 2, 3)}
    line_peer = {d: (line(d) * PLANE + q, rep) for d in (1, 2, 3)}
    core_peer = (me, 1 - rep)

    def remote(src, dst, send, recv, peer):
        return pltpu.make_async_remote_copy(
            src_ref=src, dst_ref=dst, send_sem=send, recv_sem=recv,
            device_id=peer, device_id_type=MESH,
        )

    own = gath.at[0, pl.ds(0, tile)]
    load_feat = pltpu.make_async_copy(feat, own, loc_sem.at[0])
    load_blk = pltpu.make_async_copy(blocks, blk, loc_sem.at[1])
    load_w = pltpu.make_async_copy(weight, wv, loc_sem.at[2])
    load_cot = pltpu.make_async_copy(cot, cotv, loc_sem.at[3])
    for c in (load_feat, load_blk, load_w, load_cot):
        c.start()

    barrier = pltpu.get_barrier_semaphore()
    peers = list(plane_peer.values()) + list(line_peer.values()) + [core_peer]
    for peer in peers:
        pl.semaphore_signal(barrier, inc=1, device_id=peer, device_id_type=MESH)
    pl.semaphore_wait(barrier, len(peers))
    load_feat.wait()

    def slot(j, k):
        return gath.at[j, pl.ds(pl.multiple_of(k * tile, tile), tile)]

    def half(j, k, h):
        part = tile // 2
        return gath.at[j, pl.ds(pl.multiple_of(k * tile + h * part, part), part)]

    first = 1 + 2 * (z // 2)
    second = 2 + z - 3 * (z // 2)
    order = (0, first, second, 6 - first - second)
    middle = (z + 1) // 2 == 1

    def pass_on(i, target):
        k = order[i]
        there = lax.rem(z + k - target + Z, Z)
        return remote(slot(0, k), slot(0, there), z_s.at[i], z_r.at[there], (target * PLANE + q, rep))

    up = remote(slot(0, 0), slot(0, Z - 1), z_s.at[0], z_r.at[Z - 1], ((z + 1) * PLANE + q, rep))
    down = remote(slot(0, 0), slot(0, 1), z_s.at[4], z_r.at[1], ((z - 1) * PLANE + q, rep))
    relay = {1: pass_on(1, lax.rem(3 * z + 1, Z)), 2: pass_on(2, Z - 1 - z), 3: pass_on(3, lax.rem(3 * z + 1, Z))}

    @pl.when(z < Z - 1)
    def _():
        up.start()

    @pl.when(z > 0)
    def _():
        down.start()

    x_copy = [remote(slot(0, k), slot(1, k), x_s.at[k], x_r.at[k], plane_peer[1]) for k in order]
    y_copy = [remote(slot(0, k), slot(2, k), y_s.at[k], y_r.at[k], plane_peer[2]) for k in order]
    dx_copy = [remote(half(2, k, 0), half(3, k, 0), dx_s.at[k], dx_r.at[k], plane_peer[1]) for k in order]
    dy_copy = [remote(half(1, k, 1), half(3, k, 1), dy_s.at[k], dy_r.at[k], plane_peer[2]) for k in order]
    x_copy[0].start()
    y_copy[0].start()

    def live(p):
        panel = rep if p == 0 else 1 - rep
        count = counts[panel]
        return [jnp.where(s < count, cols[panel, 0, s], -1) for s in range(cols.shape[2])]

    lists = [live(0), live(1)]
    load_blk.wait()
    for j in range(PLANE):
        for k in range(Z):
            for p in range(2):
                panel = rep if p == 0 else 1 - rep
                column = (line(k) * PLANE + flip(j)) * 2 + rep
                place = jnp.int32(0)
                for s, listed in enumerate(lists[p]):
                    place = jnp.where(listed == column, jnp.int32(s + 1), place)
                block = blk[panel, 0, jnp.maximum(place - 1, 0)]
                keep = jnp.minimum(place, 1).astype(jnp.float32).astype(jnp.bfloat16)
                dense[j, pl.ds(p * tile, tile), pl.ds(k * tile, tile)] = block * keep

    def forward(i):
        x_copy[i].wait_recv()
        dy_copy[i].start()
        y_copy[i].wait_recv()
        dx_copy[i].start()

    for i in (1, 2, 3):
        pltpu.make_async_copy(slot(0, 0), slot(0, order[i]), z_r.at[order[i]]).wait()

        @pl.when(middle)
        def _():
            relay[i].start()

        x_copy[i].start()
        y_copy[i].start()
        if i < 3:
            forward(i - 1)
    mine, theirs = pl.ds(0, tile), pl.ds(tile, tile)

    def product(j, part):
        return jnp.dot(dense[j, part], gath[j], preferred_element_type=jnp.float32)

    acc_own[...] = product(0, mine)
    acc_oth[...] = product(0, theirs)
    forward(2)
    forward(3)
    for j in (1, 2):
        acc_own[...] += product(j, mine)
        acc_oth[...] += product(j, theirs)
    for i in range(Z):
        dx_copy[i].wait_recv()
        dy_copy[i].wait_recv()
    acc_oth[...] += product(3, theirs)
    swap = remote(acc_oth, acc_in, p_s.at[0], p_r.at[0], core_peer)
    swap.start()
    acc_own[...] += product(3, mine)
    load_w.wait()
    load_cot.wait()
    swap.wait()

    agg = (acc_own[...] + acc_in[...]).astype(jnp.bfloat16)
    aggs[...] = agg
    pre = jnp.dot(agg, wv[...], preferred_element_type=jnp.float32) + bias[...]
    sig = jax.nn.sigmoid(pre)
    slope = (cotv[...].astype(jnp.float32) * (sig * (1.0 + pre * (1.0 - sig)))).astype(jnp.bfloat16)
    half_rows, columns = width // 2, width // CHUNKS
    quarter = half_rows // PLANE
    aligned = pl.multiple_of

    def grad_half(which, c):
        part = aggs[:, pl.ds(aligned(which * half_rows, half_rows), half_rows)]
        cut = slope[:, c * columns:(c + 1) * columns]
        return lax.dot_general(part, cut, (((0,), (0,)), ((), ())), preferred_element_type=jnp.float32)

    chunks = range(CHUNKS)
    pair = [remote(pair_out.at[c], pair_in.at[c], p_s.at[c + 2], p_r.at[c + 2], core_peer) for c in chunks]
    for c in chunks:
        pair_out[c] = grad_half(1 - rep, c).astype(jnp.bfloat16)
        pair[c].start()
    total = jnp.sum(slope.astype(jnp.float32), axis=0, keepdims=True)
    lanes = width // 4
    row_id = lax.broadcasted_iota(jnp.int32, (8, lanes), 0)
    spread = jnp.zeros((8, lanes), jnp.float32)
    for i in range(4):
        spread = jnp.where(row_id == i, total[:, i * lanes:(i + 1) * lanes], spread)
    ext[0] = spread
    ext_copy = remote(ext.at[0], ext_pair, p_s.at[1], p_r.at[1], core_peer)
    ext_copy.start()

    plane_sum = []
    for c in chunks:
        own_half = grad_half(rep, c)
        pair[c].wait_recv()
        both = own_half + pair_in[c].astype(jnp.float32)
        half32[c] = both
        half16[c] = both.astype(jnp.bfloat16)
        copies = []
        for j in (3, 1, 2):
            piece = half16.at[c, pl.ds(aligned(flip(j) * quarter, quarter), quarter)]
            copies.append(remote(piece, plane_in.at[c, j - 1], rs_s.at[c, j], rs_r.at[c, j], plane_peer[j]))
        for copy in copies:
            copy.start()
        plane_sum.append(copies)
    ext_copy.wait()
    ext[1] = ext[0] + ext_pair[...]
    ext_sum = [remote(ext.at[1], ext_plane.at[j - 1], e_s.at[j], e_r.at[j], plane_peer[j]) for j in (1, 2, 3)]
    for copy in ext_sum:
        copy.start()
    hidv[...] = (pre * sig).astype(jnp.bfloat16)
    store_hid = pltpu.make_async_copy(hidv, hid_out, loc_sem.at[4])
    store_hid.start()

    def region(c, core, place):
        start = core * half_rows + place * quarter
        return fin.at[c, pl.ds(aligned(start, quarter), quarter)]

    inner_peer = ((1 + z // 2) * PLANE + q, rep)
    end_peer = (lax.rem(3 * z + 1, Z) * PLANE + q, rep)
    twin = ((Z - 1 - z) * PLANE + q, rep)
    to_inner = [remote(sum16.at[c], line_in.at[c, 0], zl_s.at[c, 0], zl_r.at[c, 0], inner_peer) for c in chunks]
    to_twin = [remote(sum16.at[c], line_in.at[c, 1], zl_s.at[c, 1], zl_r.at[c, 1], twin) for c in chunks]
    to_end = [remote(region(c, rep, q), region(c, rep, q), zl_s.at[c, 2], zl_r.at[c, 2], end_peer) for c in chunks]
    for c in chunks:
        for copy in plane_sum[c]:
            copy.wait_recv()
        part = half32[c, pl.ds(aligned(q * quarter, quarter), quarter)]
        for j in range(3):
            part = part + plane_in[c, j].astype(jnp.float32)

        @pl.when(jnp.logical_not(middle))
        def _():
            sum16[c] = part.astype(jnp.bfloat16)
            to_inner[c].start()

        @pl.when(middle)
        def _():
            sum32[c] = part
    for copy in ext_sum:
        copy.wait()
    ext[2] = ext[1] + (ext_plane[0] + ext_plane[1] + ext_plane[2])
    ext_line_sum = [remote(ext.at[2], ext_line.at[Z - d - 1], e_s.at[d + 4], e_r.at[Z - d + 4], line_peer[d]) for d in (1, 2, 3)]
    for copy in ext_line_sum:
        copy.start()

    for c in chunks:

        @pl.when(middle)
        def _():
            to_inner[c].wait_recv()
            sum16[c] = (sum32[c] + line_in[c, 0].astype(jnp.float32)).astype(jnp.bfloat16)
            to_twin[c].start()

    plane_all, core_all = [], []
    for c in chunks:

        @pl.when(middle)
        def _():
            to_twin[c].wait_recv()
            both = sum16[c].astype(jnp.float32) + line_in[c, 1].astype(jnp.float32)
            region(c, rep, q)[...] = both.astype(jnp.bfloat16)
            to_end[c].start()

        @pl.when(jnp.logical_not(middle))
        def _():
            to_end[c].wait_recv()

        own_q = region(c, rep, q)
        copies = {j: remote(own_q, own_q, pg_s.at[c, j], pg_r.at[c, j], plane_peer[j]) for j in (3, 1, 2)}
        for copy in copies.values():
            copy.start()
        plane_all.append(copies)
        core_all.append(remote(own_q, own_q, cg_s.at[c, 0], cg_r.at[c, 0], core_peer))
        core_all[-1].start()
    for c in chunks:
        for j in (1, 2, 3):
            plane_all[c][j].wait_recv()
            piece = region(c, rep, flip(j))
            core_all.append(remote(piece, piece, cg_s.at[c, j], cg_r.at[c, j], core_peer))
            core_all[-1].start()
    for copy in ext_line_sum:
        copy.wait()
    everything = ext[2] + (ext_line[0] + ext_line[1] + ext_line[2])
    for i in range(4):
        bias_out[:, i * lanes:(i + 1) * lanes] = everything[i:i + 1] * factor
    for copy in core_all:
        copy.wait()
    store_wg = []
    for c in chunks:
        store_wg.append(pltpu.make_async_copy(fin.at[c], wg_out.at[:, pl.ds(c * columns, columns)], loc_sem.at[5 + c]))
        store_wg[-1].start()
    for copies in plane_sum + [list(p.values()) for p in plane_all] + [pair]:
        for copy in copies:
            copy.wait_send()

    for c in x_copy + y_copy + dx_copy + dy_copy:
        c.wait_send()

    @pl.when(z < Z - 1)
    def _():
        up.wait_send()

    @pl.when(z > 0)
    def _():
        down.wait_send()

    @pl.when(middle)
    def _():
        for c in list(relay.values()) + to_twin + to_end:
            c.wait_send()

    @pl.when(jnp.logical_not(middle))
    def _():
        for c in to_inner:
            c.wait_send()

    store_hid.wait()
    for copy in store_wg:
        copy.wait()


def finish_kernel(factor, hid, wg, bias, hid_out, wg_out, bias_out, narrow, wide, sem):
    rows = wg.shape[0] // PARTS
    cuts = [pl.ds(i * rows, rows) for i in range(PARTS)]
    loads = [pltpu.make_async_copy(wg.at[c], narrow.at[c], sem.at[2 + i]) for i, c in enumerate(cuts)]
    stores = [pltpu.make_async_copy(wide.at[c], wg_out.at[c], sem.at[2 + PARTS + i]) for i, c in enumerate(cuts)]
    others = [pltpu.make_async_copy(hid, hid_out, sem.at[0]), pltpu.make_async_copy(bias, bias_out, sem.at[1])]
    for copy in loads + others:
        copy.start()
    for i, c in enumerate(cuts):
        loads[i].wait()
        wide[c] = narrow[c].astype(jnp.float32) * factor
        stores[i].start()
    for copy in others + stores:
        copy.wait()


def fused_shards(features, col_panels, block_counts, block_values, weight, bias, cotangent):
    tile, width = features.shape
    bf16, f32 = jnp.bfloat16, jnp.float32
    half_rows, columns = width // 2, width // CHUNKS
    quarter = half_rows // PLANE
    dma = pltpu.SemaphoreType.DMA
    hbm = pl.BlockSpec(memory_space=pl.ANY)

    smem = pl.BlockSpec(memory_space=pltpu.SMEM)
    vmem = pl.BlockSpec(memory_space=pltpu.VMEM)
    factor = 1.0 / math.sqrt(lax.axis_size("section") * lax.axis_size("rep") * tile)
    hidden, weight_sum, bias_sum = pl.pallas_call(
        functools.partial(fused_kernel, factor),
        out_shape=(
            jax.ShapeDtypeStruct((tile, width), bf16),
            jax.ShapeDtypeStruct((width, width), bf16),
            jax.ShapeDtypeStruct((1, width), f32),
        ),
        in_specs=[hbm, smem, smem, hbm, hbm, vmem, hbm],
        out_specs=(hbm, hbm, vmem),
        scratch_shapes=[
            pltpu.VMEM((PLANE, Z * tile, width), bf16),
            pltpu.VMEM((PLANE, 2 * tile, Z * tile), bf16),
            pltpu.VMEM(block_values.shape, bf16),
            pltpu.VMEM((width, width), bf16),
            pltpu.VMEM((tile, width), bf16),
            pltpu.VMEM((tile, width), f32),
            pltpu.VMEM((tile, width), f32),
            pltpu.VMEM((tile, width), f32),
            pltpu.VMEM((tile, width), bf16),
            pltpu.VMEM((tile, width), bf16),
            pltpu.VMEM((CHUNKS, half_rows, columns), bf16),
            pltpu.VMEM((CHUNKS, half_rows, columns), bf16),
            pltpu.VMEM((CHUNKS, half_rows, columns), f32),
            pltpu.VMEM((CHUNKS, half_rows, columns), bf16),
            pltpu.VMEM((CHUNKS, 3, quarter, columns), bf16),
            pltpu.VMEM((CHUNKS, quarter, columns), f32),
            pltpu.VMEM((CHUNKS, quarter, columns), bf16),
            pltpu.VMEM((CHUNKS, 2, quarter, columns), bf16),
            pltpu.VMEM((CHUNKS, width, columns), bf16),
            pltpu.VMEM((3, 8, width // 4), f32),
            pltpu.VMEM((8, width // 4), f32),
            pltpu.VMEM((3, 8, width // 4), f32),
            pltpu.VMEM((3, 8, width // 4), f32),
            dma((5 + CHUNKS,)),
            dma((5,)), dma((4,)), dma((4,)), dma((4,)), dma((4,)), dma((4,)),
            dma((4,)), dma((4,)), dma((4,)), dma((4,)),
            dma((2 + CHUNKS,)), dma((2 + CHUNKS,)), dma((8,)), dma((8,)),
        ] + [dma((CHUNKS, 4))] * 8,
        compiler_params=pltpu.CompilerParams(
            collective_id=0, has_side_effects=True, vmem_limit_bytes=60 * 1024 * 1024
        ),
        name="fused_layer",
    )(features, col_panels, block_counts.reshape(-1), block_values, weight, bias.reshape(1, width), cotangent)
    hidden, weight_grad, bias_grad = pl.pallas_call(
        functools.partial(finish_kernel, factor),
        out_shape=(
            jax.ShapeDtypeStruct((tile, width), bf16),
            jax.ShapeDtypeStruct((width, width), f32),
            jax.ShapeDtypeStruct((1, width), f32),
        ),
        in_specs=[hbm, hbm, hbm],
        out_specs=(hbm, hbm, hbm),
        scratch_shapes=[
            pltpu.VMEM((width, width), bf16), pltpu.VMEM((width, width), f32),
            dma((2 + 2 * PARTS,)),
        ],
        compiler_params=pltpu.CompilerParams(vmem_limit_bytes=60 * 1024 * 1024),
        name="finish",
    )(hidden, weight_sum, bias_sum)
    return hidden, weight_grad, bias_grad.reshape(width)


def fits_fused(mesh):
    return dict(mesh.shape) == {"section": Z * PLANE, "rep": 2}


def solution(mesh):
    in_specs = (
        P(("section", "rep"), None),
        P("section", "rep", None),
        P("section", "rep"),
        P("section", "rep", None, None, None),
        P(),
        P(),
        P(("section", "rep"), None),
    )
    out_specs = (P(("section", "rep"), None), P(), P())
    body = fused_shards if fits_fused(mesh) else shards
    return jax.shard_map(body, mesh=mesh, in_specs=in_specs, out_specs=out_specs, check_vma=False)
```

```python
import functools
import math

import jax
import jax.numpy as jnp
from jax import lax
from jax.experimental import pallas as pl
from jax.experimental.pallas import tpu as pltpu
from jax.sharding import PartitionSpec as P


def shards(features, col_panels, block_counts, block_values, weight, bias, cotangent):
    rep_count = lax.axis_size("rep")
    rep_index = lax.axis_index("rep")
    tile_size = block_values.shape[-1]
    feat_width = features.shape[1]
    own_panels = features.shape[0] // tile_size
    row_panels = col_panels.shape[0]
    slot_count = col_panels.shape[2]
    global_cols = col_panels[:, 0, :]
    local_cols = global_cols // (own_panels * rep_count) * own_panels + global_cols % own_panels
    live_counts = block_counts[:, 0]
    slot_mask = jnp.arange(slot_count, dtype=jnp.int32)[None, :] < live_counts[:, None]
    tiles = block_values[:, 0]
    empty = jnp.zeros((row_panels, tile_size, feat_width), jnp.float32)
    gathered = lax.all_gather(features, "section", axis=0, tiled=True)
    all_panels = gathered.reshape(-1, tile_size, feat_width)
    slot_step = 4
    turn_count = (jnp.max(live_counts) + slot_step - 1) // slot_step

    def one_turn(turn, running):
        begin_slot = turn * slot_step
        step_cols = lax.dynamic_slice_in_dim(local_cols, begin_slot, slot_step, 1)
        step_mask = lax.dynamic_slice_in_dim(slot_mask, begin_slot, slot_step, 1)
        step_tiles = lax.dynamic_slice_in_dim(tiles, begin_slot, slot_step, 1)
        step_tiles = jnp.where(step_mask[:, :, None, None], step_tiles, jnp.zeros((), jnp.bfloat16))
        picked = all_panels[step_cols]
        return running + jnp.einsum(
            "gkab,gkbf->gaf", step_tiles, picked, preferred_element_type=jnp.float32
        )

    gathered_sum = lax.fori_loop(0, turn_count, one_turn, empty)
    partial_value = gathered_sum.reshape(row_panels * tile_size, feat_width)
    own_rows = own_panels * tile_size
    summed_all = lax.psum(partial_value, "rep")
    summed_own = lax.dynamic_slice_in_dim(summed_all, rep_index * own_rows, own_rows, 0)
    aggregated = summed_own.astype(jnp.bfloat16)
    pre = jnp.dot(aggregated, weight, preferred_element_type=jnp.float32) + bias
    hidden = jax.nn.silu(pre).astype(jnp.bfloat16)
    sigmoid_pre = jax.nn.sigmoid(pre)
    slope = (
        cotangent.astype(jnp.float32) * (sigmoid_pre * (1.0 + pre * (1.0 - sigmoid_pre)))
    ).astype(jnp.bfloat16)
    local_weight = jnp.einsum("nd,nf->df", aggregated, slope, preferred_element_type=jnp.float32)
    local_bias = jnp.sum(slope.astype(jnp.float32), axis=0)
    weight_sum, bias_sum = lax.psum((local_weight, local_bias), ("section", "rep"))
    node_total = lax.axis_size("section") * rep_count * own_rows
    factor = 1.0 / math.sqrt(node_total)
    return (hidden, weight_sum * factor, bias_sum * factor)

MESH = pl.DeviceIdType.MESH
Z, PLANE = 4, 4
CHUNKS = 2


def fused_kernel(
    factor,
    feat, cols, counts, blocks, weight, bias, cot,
    hid_out, wg_out, bias_out,
    gath, dense, blk, wv, cotv, acc_own, acc_oth, acc_in, aggs, hidv,
    pair_out, pair_in, half32, half16, plane_in, sum32, sum16, line_in, fin,
    ext, ext_pair, ext_plane, ext_line,
    loc_sem, z_s, z_r, x_s, x_r, y_s, y_r, dx_s, dx_r, dy_s, dy_r,
    p_s, p_r, e_s, e_r, rs_s, rs_r, zl_s, zl_r, zg_s, zg_r, pg_s, pg_r, cg_s, cg_r,
):
    tile, width = feat.shape
    me, rep = lax.axis_index("section"), lax.axis_index("rep")
    z, q = me // PLANE, me % PLANE
    y, x = q // 2, q % 2

    def flip(j):
        return (1 - y if j & 2 else y) * 2 + (1 - x if j & 1 else x)

    def line(d):
        return lax.rem(z + d, Z)

    plane_peer = {j: (z * PLANE + flip(j), rep) for j in (1, 2, 3)}
    line_peer = {d: (line(d) * PLANE + q, rep) for d in (1, 2, 3)}
    core_peer = (me, 1 - rep)

    def remote(src, dst, send, recv, peer):
        return pltpu.make_async_remote_copy(
            src_ref=src, dst_ref=dst, send_sem=send, recv_sem=recv,
            device_id=peer, device_id_type=MESH,
        )

    own = gath.at[0, pl.ds(0, tile)]
    load_feat = pltpu.make_async_copy(feat, own, loc_sem.at[0])
    load_blk = pltpu.make_async_copy(blocks, blk, loc_sem.at[1])
    load_w = pltpu.make_async_copy(weight, wv, loc_sem.at[2])
    load_cot = pltpu.make_async_copy(cot, cotv, loc_sem.at[3])
    for c in (load_feat, load_blk, load_w, load_cot):
        c.start()

    barrier = pltpu.get_barrier_semaphore()
    peers = list(plane_peer.values()) + list(line_peer.values()) + [core_peer]
    for peer in peers:
        pl.semaphore_signal(barrier, inc=1, device_id=peer, device_id_type=MESH)
    pl.semaphore_wait(barrier, len(peers))
    load_feat.wait()

    def slot(j, k):
        return gath.at[j, pl.ds(pl.multiple_of(k * tile, tile), tile)]

    def half(j, k, h):
        part = tile // 2
        return gath.at[j, pl.ds(pl.multiple_of(k * tile + h * part, part), part)]

    first = 1 + 2 * (z // 2)
    second = 2 + z - 3 * (z // 2)
    order = (0, first, second, 6 - first - second)
    middle = (z + 1) // 2 == 1

    cross = tile - tile // 4

    def piece(j, k):
        start, count = (0, tile) if j == 0 else (cross, tile - cross)
        return gath.at[j, pl.ds(pl.multiple_of(k * tile + start, 16), count)]

    def head(j, k):
        return gath.at[j, pl.ds(pl.multiple_of(k * tile, tile), cross)]

    def pass_on(j, i, target):
        k = order[i]
        there = lax.rem(z + k - target + Z, Z)
        return remote(piece(j, k), piece(j, there), z_s.at[j, i], z_r.at[j, there], (target * PLANE + q, rep))

    up = [remote(piece(j, 0), piece(j, Z - 1), z_s.at[j, 0], z_r.at[j, Z - 1], ((z + 1) * PLANE + q, rep)) for j in range(3)]
    down = [remote(piece(j, 0), piece(j, 1), z_s.at[j, 4], z_r.at[j, 1], ((z - 1) * PLANE + q, rep)) for j in range(3)]
    outer, inner = lax.rem(3 * z + 1, Z), Z - 1 - z
    relay = [{1: pass_on(j, 1, outer), 2: pass_on(j, 2, inner), 3: pass_on(j, 3, outer)} for j in range(3)]

    def send_along(j):
        @pl.when(z < Z - 1)
        def _():
            up[j].start()

        @pl.when(z > 0)
        def _():
            down[j].start()

    def relay_along(j, i):
        pltpu.make_async_copy(piece(j, 0), piece(j, order[i]), z_r.at[j, order[i]]).wait()

        @pl.when(middle)
        def _():
            relay[j][i].start()

    send_along(0)

    def across(j, i):
        k = order[i]
        send, recv = ((x_s, x_r), (y_s, y_r))[j - 1]
        part = slot if i == 0 else head
        return remote(part(0, k), part(j, k), send.at[k], recv.at[k], plane_peer[j])

    x_copy = [across(1, i) for i in range(Z)]
    y_copy = [across(2, i) for i in range(Z)]
    dx_copy = [remote(half(2, k, 0), half(3, k, 0), dx_s.at[k], dx_r.at[k], plane_peer[1]) for k in order]
    dy_copy = [remote(half(1, k, 1), half(3, k, 1), dy_s.at[k], dy_r.at[k], plane_peer[2]) for k in order]
    x_copy[0].start()
    y_copy[0].start()

    def live(p):
        panel = rep if p == 0 else 1 - rep
        count = counts[panel]
        return [jnp.where(s < count, cols[panel, 0, s], -1) for s in range(cols.shape[2])]

    lists = [live(0), live(1)]
    load_blk.wait()
    for j in range(PLANE):
        for k in range(Z):
            for p in range(2):
                panel = rep if p == 0 else 1 - rep
                column = (line(k) * PLANE + flip(j)) * 2 + rep
                place = jnp.int32(0)
                for s, listed in enumerate(lists[p]):
                    place = jnp.where(listed == column, jnp.int32(s + 1), place)
                block = blk[panel, 0, jnp.maximum(place - 1, 0)]
                keep = jnp.minimum(place, 1).astype(jnp.float32).astype(jnp.bfloat16)
                dense[j, pl.ds(p * tile, tile), pl.ds(k * tile, tile)] = block * keep

    def forward(i):
        y_copy[i].wait_recv()
        if i == 0:
            send_along(2)
        dx_copy[i].start()
        x_copy[i].wait_recv()
        if i == 0:
            send_along(1)
        else:
            relay_along(1, i)
        dy_copy[i].start()
        if i:
            relay_along(2, i)

    for i in (1, 2, 3):
        relay_along(0, i)
        x_copy[i].start()
        y_copy[i].start()
        if i < 3:
            forward(i - 1)
    mine, theirs = pl.ds(0, tile), pl.ds(tile, tile)

    def product(j, part):
        return jnp.dot(dense[j, part], gath[j], preferred_element_type=jnp.float32)

    acc_own[...] = product(0, mine)
    acc_oth[...] = product(0, theirs)
    forward(2)
    forward(3)
    for j in (1, 2):
        acc_own[...] += product(j, mine)
        acc_oth[...] += product(j, theirs)
    for i in range(Z):
        dx_copy[i].wait_recv()
        dy_copy[i].wait_recv()
    acc_oth[...] += product(3, theirs)
    swap = remote(acc_oth, acc_in, p_s.at[0], p_r.at[0], core_peer)
    swap.start()
    acc_own[...] += product(3, mine)
    load_w.wait()
    load_cot.wait()
    swap.wait()

    agg = (acc_own[...] + acc_in[...]).astype(jnp.bfloat16)
    aggs[...] = agg
    pre = jnp.dot(agg, wv[...], preferred_element_type=jnp.float32) + bias[...]
    sig = jax.nn.sigmoid(pre)
    slope = (cotv[...].astype(jnp.float32) * (sig * (1.0 + pre * (1.0 - sig)))).astype(jnp.bfloat16)
    half_rows, columns = width // 2, width // CHUNKS
    quarter = half_rows // PLANE
    share = quarter // Z
    aligned = pl.multiple_of

    def grad_half(which, c):
        part = aggs[:, pl.ds(aligned(which * half_rows, half_rows), half_rows)]
        cut = slope[:, c * columns:(c + 1) * columns]
        return lax.dot_general(part, cut, (((0,), (0,)), ((), ())), preferred_element_type=jnp.float32)

    chunks = range(CHUNKS)
    pair = [remote(pair_out.at[c], pair_in.at[c], p_s.at[c + 2], p_r.at[c + 2], core_peer) for c in chunks]
    for c in chunks:
        pair_out[c] = grad_half(1 - rep, c).astype(jnp.bfloat16)
        pair[c].start()
    total = jnp.sum(slope.astype(jnp.float32), axis=0, keepdims=True)
    lanes = width // 4
    row_id = lax.broadcasted_iota(jnp.int32, (8, lanes), 0)
    spread = jnp.zeros((8, lanes), jnp.float32)
    for i in range(4):
        spread = jnp.where(row_id == i, total[:, i * lanes:(i + 1) * lanes], spread)
    ext[0] = spread
    ext_copy = remote(ext.at[0], ext_pair, p_s.at[1], p_r.at[1], core_peer)
    ext_copy.start()

    plane_sum = []
    for c in chunks:
        own_half = grad_half(rep, c)
        pair[c].wait_recv()
        both = own_half + pair_in[c].astype(jnp.float32)
        half32[c] = both
        half16[c] = both.astype(jnp.bfloat16)
        copies = []
        for j in (3, 1, 2):
            piece = half16.at[c, pl.ds(aligned(flip(j) * quarter, quarter), quarter)]
            copies.append(remote(piece, plane_in.at[c, j - 1], rs_s.at[c, j], rs_r.at[c, j], plane_peer[j]))
        for copy in copies:
            copy.start()
        plane_sum.append(copies)
    ext_copy.wait()
    ext[1] = ext[0] + ext_pair[...]
    ext_sum = [remote(ext.at[1], ext_plane.at[j - 1], e_s.at[j], e_r.at[j], plane_peer[j]) for j in (1, 2, 3)]
    for copy in ext_sum:
        copy.start()
    hidv[...] = (pre * sig).astype(jnp.bfloat16)
    store_hid = pltpu.make_async_copy(hidv, hid_out, loc_sem.at[4])
    store_hid.start()

    line_sum = []
    for c in chunks:
        for copy in plane_sum[c]:
            copy.wait_recv()
        part = half32[c, pl.ds(aligned(q * quarter, quarter), quarter)]
        for j in range(3):
            part = part + plane_in[c, j].astype(jnp.float32)
        sum32[c] = part
        sum16[c] = part.astype(jnp.bfloat16)
        copies = []
        for d in (2, 1, 3):
            piece = sum16.at[c, pl.ds(aligned(line(d) * share, share), share)]
            copies.append(remote(piece, line_in.at[c, Z - d - 1], zl_s.at[c, d], zl_r.at[c, Z - d], line_peer[d]))
        for copy in copies:
            copy.start()
        line_sum.append(copies)
    for copy in ext_sum:
        copy.wait()
    ext[2] = ext[1] + (ext_plane[0] + ext_plane[1] + ext_plane[2])
    ext_line_sum = [remote(ext.at[2], ext_line.at[Z - d - 1], e_s.at[d + 4], e_r.at[Z - d + 4], line_peer[d]) for d in (1, 2, 3)]
    for copy in ext_line_sum:
        copy.start()

    def region(c, core, place, height, count):
        start = core * half_rows + place * quarter + height * share
        return fin.at[c, pl.ds(aligned(start, share), count)]

    line_all = []
    for c in chunks:
        for copy in line_sum[c]:
            copy.wait_recv()
        part = sum32[c, pl.ds(aligned(z * share, share), share)]
        for d in range(3):
            part = part + line_in[c, d].astype(jnp.float32)
        here = region(c, rep, q, z, share)
        here[...] = part.astype(jnp.bfloat16)
        copies = [remote(here, here, zg_s.at[c, d], zg_r.at[c, Z - d], line_peer[d]) for d in (2, 1, 3)]
        for copy in copies:
            copy.start()
        line_all.append(copies)
    for copy in ext_line_sum:
        copy.wait()
    everything = ext[2] + (ext_line[0] + ext_line[1] + ext_line[2])
    for i in range(4):
        bias_out[:, i * lanes:(i + 1) * lanes] = everything[i:i + 1] * factor
    plane_all, core_all = [], []
    for c in chunks:
        for copy in line_all[c]:
            copy.wait_recv()
        own_q = region(c, rep, q, 0, quarter)
        copies = {j: remote(own_q, own_q, pg_s.at[c, j], pg_r.at[c, j], plane_peer[j]) for j in (3, 1, 2)}
        for copy in copies.values():
            copy.start()
        plane_all.append(copies)
        core_all.append(remote(own_q, own_q, cg_s.at[c, 0], cg_r.at[c, 0], core_peer))
        core_all[-1].start()
    for c in chunks:
        for j in (1, 2, 3):
            plane_all[c][j].wait_recv()
            piece = region(c, rep, flip(j), 0, quarter)
            core_all.append(remote(piece, piece, cg_s.at[c, j], cg_r.at[c, j], core_peer))
            core_all[-1].start()
    for copy in core_all:
        copy.wait()
    store_wg = []
    for c in chunks:
        store_wg.append(pltpu.make_async_copy(fin.at[c], wg_out.at[:, pl.ds(c * columns, columns)], loc_sem.at[5 + c]))
        store_wg[-1].start()
    for copies in plane_sum + line_sum + line_all + [list(p.values()) for p in plane_all] + [pair]:
        for copy in copies:
            copy.wait_send()

    for c in x_copy + y_copy + dx_copy + dy_copy:
        c.wait_send()

    @pl.when(z < Z - 1)
    def _():
        for c in up:
            c.wait_send()

    @pl.when(z > 0)
    def _():
        for c in down:
            c.wait_send()

    @pl.when(middle)
    def _():
        for j in range(3):
            for c in relay[j].values():
                c.wait_send()

    store_hid.wait()
    for copy in store_wg:
        copy.wait()


def fused_shards(features, col_panels, block_counts, block_values, weight, bias, cotangent):
    tile, width = features.shape
    bf16, f32 = jnp.bfloat16, jnp.float32
    half_rows, columns = width // 2, width // CHUNKS
    quarter = half_rows // PLANE
    share = quarter // Z
    dma = pltpu.SemaphoreType.DMA
    hbm = pl.BlockSpec(memory_space=pl.ANY)

    smem = pl.BlockSpec(memory_space=pltpu.SMEM)
    vmem = pl.BlockSpec(memory_space=pltpu.VMEM)
    factor = 1.0 / math.sqrt(lax.axis_size("section") * lax.axis_size("rep") * tile)
    hidden, weight_sum, bias_sum = pl.pallas_call(
        functools.partial(fused_kernel, factor),
        out_shape=(
            jax.ShapeDtypeStruct((tile, width), bf16),
            jax.ShapeDtypeStruct((width, width), bf16),
            jax.ShapeDtypeStruct((1, width), f32),
        ),
        in_specs=[hbm, smem, smem, hbm, hbm, vmem, hbm],
        out_specs=(hbm, hbm, vmem),
        scratch_shapes=[
            pltpu.VMEM((PLANE, Z * tile, width), bf16),
            pltpu.VMEM((PLANE, 2 * tile, Z * tile), bf16),
            pltpu.VMEM(block_values.shape, bf16),
            pltpu.VMEM((width, width), bf16),
            pltpu.VMEM((tile, width), bf16),
            pltpu.VMEM((tile, width), f32),
            pltpu.VMEM((tile, width), f32),
            pltpu.VMEM((tile, width), f32),
            pltpu.VMEM((tile, width), bf16),
            pltpu.VMEM((tile, width), bf16),
            pltpu.VMEM((CHUNKS, half_rows, columns), bf16),
            pltpu.VMEM((CHUNKS, half_rows, columns), bf16),
            pltpu.VMEM((CHUNKS, half_rows, columns), f32),
            pltpu.VMEM((CHUNKS, half_rows, columns), bf16),
            pltpu.VMEM((CHUNKS, 3, quarter, columns), bf16),
            pltpu.VMEM((CHUNKS, quarter, columns), f32),
            pltpu.VMEM((CHUNKS, quarter, columns), bf16),
            pltpu.VMEM((CHUNKS, 3, share, columns), bf16),
            pltpu.VMEM((CHUNKS, width, columns), bf16),
            pltpu.VMEM((3, 8, width // 4), f32),
            pltpu.VMEM((8, width // 4), f32),
            pltpu.VMEM((3, 8, width // 4), f32),
            pltpu.VMEM((3, 8, width // 4), f32),
            dma((5 + CHUNKS,)),
            dma((3, 5)), dma((3, 4)), dma((4,)), dma((4,)), dma((4,)), dma((4,)),
            dma((4,)), dma((4,)), dma((4,)), dma((4,)),
            dma((2 + CHUNKS,)), dma((2 + CHUNKS,)), dma((8,)), dma((8,)),
        ] + [dma((CHUNKS, 4))] * 10,
        compiler_params=pltpu.CompilerParams(
            collective_id=0, has_side_effects=True, vmem_limit_bytes=60 * 1024 * 1024
        ),
        name="fused_layer",
    )(features, col_panels, block_counts.reshape(-1), block_values, weight, bias.reshape(1, width), cotangent)
    return hidden, weight_sum.astype(f32) * factor, bias_sum[0]


def fits_fused(mesh):
    return dict(mesh.shape) == {"section": Z * PLANE, "rep": 2}


def solution(mesh):
    in_specs = (
        P(("section", "rep"), None),
        P("section", "rep", None),
        P("section", "rep"),
        P("section", "rep", None, None, None),
        P(),
        P(),
        P(("section", "rep"), None),
    )
    out_specs = (P(("section", "rep"), None), P(), P())
    body = fused_shards if fits_fused(mesh) else shards
    return jax.shard_map(body, mesh=mesh, in_specs=in_specs, out_specs=out_specs, check_vma=False)
```

```python
import functools
import math

import jax
import jax.numpy as jnp
from jax import lax
from jax.experimental import pallas as pl
from jax.experimental.pallas import tpu as pltpu
from jax.sharding import PartitionSpec as P


def shards(features, col_panels, block_counts, block_values, weight, bias, cotangent):
    rep_count = lax.axis_size("rep")
    rep_index = lax.axis_index("rep")
    tile_size = block_values.shape[-1]
    feat_width = features.shape[1]
    own_panels = features.shape[0] // tile_size
    row_panels = col_panels.shape[0]
    slot_count = col_panels.shape[2]
    global_cols = col_panels[:, 0, :]
    local_cols = global_cols // (own_panels * rep_count) * own_panels + global_cols % own_panels
    live_counts = block_counts[:, 0]
    slot_mask = jnp.arange(slot_count, dtype=jnp.int32)[None, :] < live_counts[:, None]
    tiles = block_values[:, 0]
    empty = jnp.zeros((row_panels, tile_size, feat_width), jnp.float32)
    gathered = lax.all_gather(features, "section", axis=0, tiled=True)
    all_panels = gathered.reshape(-1, tile_size, feat_width)
    slot_step = 4
    turn_count = (jnp.max(live_counts) + slot_step - 1) // slot_step

    def one_turn(turn, running):
        begin_slot = turn * slot_step
        step_cols = lax.dynamic_slice_in_dim(local_cols, begin_slot, slot_step, 1)
        step_mask = lax.dynamic_slice_in_dim(slot_mask, begin_slot, slot_step, 1)
        step_tiles = lax.dynamic_slice_in_dim(tiles, begin_slot, slot_step, 1)
        step_tiles = jnp.where(step_mask[:, :, None, None], step_tiles, jnp.zeros((), jnp.bfloat16))
        picked = all_panels[step_cols]
        return running + jnp.einsum(
            "gkab,gkbf->gaf", step_tiles, picked, preferred_element_type=jnp.float32
        )

    gathered_sum = lax.fori_loop(0, turn_count, one_turn, empty)
    partial_value = gathered_sum.reshape(row_panels * tile_size, feat_width)
    own_rows = own_panels * tile_size
    summed_all = lax.psum(partial_value, "rep")
    summed_own = lax.dynamic_slice_in_dim(summed_all, rep_index * own_rows, own_rows, 0)
    aggregated = summed_own.astype(jnp.bfloat16)
    pre = jnp.dot(aggregated, weight, preferred_element_type=jnp.float32) + bias
    hidden = jax.nn.silu(pre).astype(jnp.bfloat16)
    sigmoid_pre = jax.nn.sigmoid(pre)
    slope = (
        cotangent.astype(jnp.float32) * (sigmoid_pre * (1.0 + pre * (1.0 - sigmoid_pre)))
    ).astype(jnp.bfloat16)
    local_weight = jnp.einsum("nd,nf->df", aggregated, slope, preferred_element_type=jnp.float32)
    local_bias = jnp.sum(slope.astype(jnp.float32), axis=0)
    weight_sum, bias_sum = lax.psum((local_weight, local_bias), ("section", "rep"))
    node_total = lax.axis_size("section") * rep_count * own_rows
    factor = 1.0 / math.sqrt(node_total)
    return (hidden, weight_sum * factor, bias_sum * factor)

MESH = pl.DeviceIdType.MESH
Z, PLANE = 4, 4
CHUNKS = 2


def fused_kernel(
    factor,
    feat, cols, counts, blocks, weight, bias, cot,
    hid_out, wg_out, bias_out,
    gath, dense, blk, wv, cotv, acc_own, acc_oth, acc_in, aggs, hidv,
    pair_out, pair_in, half32, half16, plane_in, sum32, sum16, line_in, fin,
    ext, ext_pair, ext_plane, ext_line,
    loc_sem, z_s, z_r, x_s, x_r, y_s, y_r, dx_s, dx_r, dy_s, dy_r,
    p_s, p_r, e_s, e_r, rs_s, rs_r, zl_s, zl_r, zg_s, zg_r, pg_s, pg_r, cg_s, cg_r,
):
    tile, width = feat.shape
    me, rep = lax.axis_index("section"), lax.axis_index("rep")
    z, q = me // PLANE, me % PLANE
    y, x = q // 2, q % 2

    def flip(j):
        return (1 - y if j & 2 else y) * 2 + (1 - x if j & 1 else x)

    def line(d):
        return lax.rem(z + d, Z)

    plane_peer = {j: (z * PLANE + flip(j), rep) for j in (1, 2, 3)}
    line_peer = {d: (line(d) * PLANE + q, rep) for d in (1, 2, 3)}
    core_peer = (me, 1 - rep)

    def remote(src, dst, send, recv, peer):
        return pltpu.make_async_remote_copy(
            src_ref=src, dst_ref=dst, send_sem=send, recv_sem=recv,
            device_id=peer, device_id_type=MESH,
        )

    own = gath.at[0, pl.ds(0, tile)]
    load_feat = pltpu.make_async_copy(feat, own, loc_sem.at[0])
    load_blk = pltpu.make_async_copy(blocks, blk, loc_sem.at[1])
    load_w = pltpu.make_async_copy(weight, wv, loc_sem.at[2])
    load_cot = pltpu.make_async_copy(cot, cotv, loc_sem.at[3])
    for c in (load_feat, load_blk, load_w, load_cot):
        c.start()

    barrier = pltpu.get_barrier_semaphore()
    peers = list(plane_peer.values()) + list(line_peer.values()) + [core_peer]
    for peer in peers:
        pl.semaphore_signal(barrier, inc=1, device_id=peer, device_id_type=MESH)
    pl.semaphore_wait(barrier, len(peers))
    load_feat.wait()

    def slot(j, k):
        return gath.at[j, pl.ds(pl.multiple_of(k * tile, tile), tile)]

    def half(j, k, h):
        part = tile // 2
        return gath.at[j, pl.ds(pl.multiple_of(k * tile + h * part, part), part)]

    first = 1 + 2 * (z // 2)
    second = 2 + z - 3 * (z // 2)
    order = (0, first, second, 6 - first - second)
    middle = (z + 1) // 2 == 1

    def pass_on(i, h, target):
        k = order[i]
        there = lax.rem(z + k - target + Z, Z)
        return remote(half(0, k, h), half(0, there, h), z_s.at[h, i], z_r.at[h, there], (target * PLANE + q, rep))

    up = [remote(half(0, 0, h), half(0, Z - 1, h), z_s.at[h, 0], z_r.at[h, Z - 1], ((z + 1) * PLANE + q, rep)) for h in range(2)]
    down = [remote(half(0, 0, h), half(0, 1, h), z_s.at[h, 4], z_r.at[h, 1], ((z - 1) * PLANE + q, rep)) for h in range(2)]
    outer, inner = lax.rem(3 * z + 1, Z), Z - 1 - z
    relay = [{1: pass_on(1, h, outer), 2: pass_on(2, h, inner), 3: pass_on(3, h, outer)} for h in range(2)]

    def across(j, i, h):
        k = order[i]
        send, recv = ((x_s, x_r), (y_s, y_r))[j - 1]
        return remote(half(0, k, h), half(j, k, h), send.at[h, k], recv.at[h, k], plane_peer[j])

    x_copy = [[across(1, i, h) for h in range(2)] for i in range(Z)]
    y_copy = [[across(2, i, h) for h in range(2)] for i in range(Z)]
    for h in range(2):
        x_copy[0][1 - h].start()
        y_copy[0][h].start()

        @pl.when(z < Z - 1)
        def _():
            up[h].start()

        @pl.when(z > 0)
        def _():
            down[h].start()

    dx_copy = [remote(half(2, k, 0), half(3, k, 0), dx_s.at[k], dx_r.at[k], plane_peer[1]) for k in order]
    dy_copy = [remote(half(1, k, 1), half(3, k, 1), dy_s.at[k], dy_r.at[k], plane_peer[2]) for k in order]
    def live(p):
        panel = rep if p == 0 else 1 - rep
        count = counts[panel]
        return [jnp.where(s < count, cols[panel, 0, s], -1) for s in range(cols.shape[2])]

    lists = [live(0), live(1)]
    load_blk.wait()
    for j in range(PLANE):
        for k in range(Z):
            for p in range(2):
                panel = rep if p == 0 else 1 - rep
                column = (line(k) * PLANE + flip(j)) * 2 + rep
                place = jnp.int32(0)
                for s, listed in enumerate(lists[p]):
                    place = jnp.where(listed == column, jnp.int32(s + 1), place)
                block = blk[panel, 0, jnp.maximum(place - 1, 0)]
                keep = jnp.minimum(place, 1).astype(jnp.float32).astype(jnp.bfloat16)
                dense[j, pl.ds(p * tile, tile), pl.ds(k * tile, tile)] = block * keep

    def forward(i):
        x_copy[i][1].wait_recv()
        dy_copy[i].start()
        y_copy[i][0].wait_recv()
        dx_copy[i].start()

    for i in (1, 2, 3):
        for h in range(2):
            k = order[i]
            pltpu.make_async_copy(half(0, 0, h), half(0, k, h), z_r.at[h, k]).wait()

            @pl.when(middle)
            def _():
                relay[h][i].start()

            (y_copy if h == 0 else x_copy)[i][h].start()
        x_copy[i][0].start()
        y_copy[i][1].start()
        forward(i - 1)
    mine, theirs = pl.ds(0, tile), pl.ds(tile, tile)

    def product(j, part):
        return jnp.dot(dense[j, part], gath[j], preferred_element_type=jnp.float32)

    def corner(i, part):
        at = pl.ds(pl.multiple_of(order[i] * tile, tile), tile)
        return jnp.dot(dense[3, part, at], gath[3, at], preferred_element_type=jnp.float32)

    acc_own[...] = product(0, mine)
    acc_oth[...] = product(0, theirs)
    forward(3)
    for i in range(Z):
        x_copy[i][0].wait_recv()
        y_copy[i][1].wait_recv()
    for j in (1, 2):
        acc_own[...] += product(j, mine)
        acc_oth[...] += product(j, theirs)
    for i in range(Z):
        dx_copy[i].wait_recv()
        dy_copy[i].wait_recv()
        acc_oth[...] += corner(i, theirs)
        if i < Z - 1:
            acc_own[...] += corner(i, mine)
    swap = remote(acc_oth, acc_in, p_s.at[0], p_r.at[0], core_peer)
    swap.start()
    acc_own[...] += corner(Z - 1, mine)
    load_w.wait()
    load_cot.wait()
    swap.wait()

    agg = (acc_own[...] + acc_in[...]).astype(jnp.bfloat16)
    aggs[...] = agg
    pre = jnp.dot(agg, wv[...], preferred_element_type=jnp.float32) + bias[...]
    sig = jax.nn.sigmoid(pre)
    slope = (cotv[...].astype(jnp.float32) * (sig * (1.0 + pre * (1.0 - sig)))).astype(jnp.bfloat16)
    half_rows, columns = width // 2, width // CHUNKS
    quarter = half_rows // PLANE
    share = quarter // Z
    aligned = pl.multiple_of

    def grad_half(which, c):
        part = aggs[:, pl.ds(aligned(which * half_rows, half_rows), half_rows)]
        cut = slope[:, c * columns:(c + 1) * columns]
        return lax.dot_general(part, cut, (((0,), (0,)), ((), ())), preferred_element_type=jnp.float32)

    chunks = range(CHUNKS)
    pair = [remote(pair_out.at[c], pair_in.at[c], p_s.at[c + 2], p_r.at[c + 2], core_peer) for c in chunks]
    for c in chunks:
        pair_out[c] = grad_half(1 - rep, c).astype(jnp.bfloat16)
        pair[c].start()
    total = jnp.sum(slope.astype(jnp.float32), axis=0, keepdims=True)
    lanes = width // 4
    row_id = lax.broadcasted_iota(jnp.int32, (8, lanes), 0)
    spread = jnp.zeros((8, lanes), jnp.float32)
    for i in range(4):
        spread = jnp.where(row_id == i, total[:, i * lanes:(i + 1) * lanes], spread)
    ext[0] = spread
    ext_copy = remote(ext.at[0], ext_pair, p_s.at[1], p_r.at[1], core_peer)
    ext_copy.start()

    plane_sum = []
    for c in chunks:
        own_half = grad_half(rep, c)
        pair[c].wait_recv()
        both = own_half + pair_in[c].astype(jnp.float32)
        half32[c] = both
        half16[c] = both.astype(jnp.bfloat16)
        copies = []
        for j in (3, 1, 2):
            piece = half16.at[c, pl.ds(aligned(flip(j) * quarter, quarter), quarter)]
            copies.append(remote(piece, plane_in.at[c, j - 1], rs_s.at[c, j], rs_r.at[c, j], plane_peer[j]))
        for copy in copies:
            copy.start()
        plane_sum.append(copies)
    ext_copy.wait()
    ext[1] = ext[0] + ext_pair[...]
    ext_sum = [remote(ext.at[1], ext_plane.at[j - 1], e_s.at[j], e_r.at[j], plane_peer[j]) for j in (1, 2, 3)]
    for copy in ext_sum:
        copy.start()
    hidv[...] = (pre * sig).astype(jnp.bfloat16)
    store_hid = pltpu.make_async_copy(hidv, hid_out, loc_sem.at[4])
    store_hid.start()

    line_sum = []
    for c in chunks:
        for copy in plane_sum[c]:
            copy.wait_recv()
        part = half32[c, pl.ds(aligned(q * quarter, quarter), quarter)]
        for j in range(3):
            part = part + plane_in[c, j].astype(jnp.float32)
        sum32[c] = part
        sum16[c] = part.astype(jnp.bfloat16)
        copies = []
        for d in (2, 1, 3):
            piece = sum16.at[c, pl.ds(aligned(line(d) * share, share), share)]
            copies.append(remote(piece, line_in.at[c, Z - d - 1], zl_s.at[c, d], zl_r.at[c, Z - d], line_peer[d]))
        for copy in copies:
            copy.start()
        line_sum.append(copies)
    for copy in ext_sum:
        copy.wait()
    ext[2] = ext[1] + (ext_plane[0] + ext_plane[1] + ext_plane[2])
    ext_line_sum = [remote(ext.at[2], ext_line.at[Z - d - 1], e_s.at[d + 4], e_r.at[Z - d + 4], line_peer[d]) for d in (1, 2, 3)]
    for copy in ext_line_sum:
        copy.start()

    def region(c, core, place, height, count):
        start = core * half_rows + place * quarter + height * share
        return fin.at[c, pl.ds(aligned(start, share), count)]

    line_all = []
    for c in chunks:
        for copy in line_sum[c]:
            copy.wait_recv()
        part = sum32[c, pl.ds(aligned(z * share, share), share)]
        for d in range(3):
            part = part + line_in[c, d].astype(jnp.float32)
        here = region(c, rep, q, z, share)
        here[...] = part.astype(jnp.bfloat16)
        copies = [remote(here, here, zg_s.at[c, d], zg_r.at[c, Z - d], line_peer[d]) for d in (2, 1, 3)]
        for copy in copies:
            copy.start()
        line_all.append(copies)
    for copy in ext_line_sum:
        copy.wait()
    everything = ext[2] + (ext_line[0] + ext_line[1] + ext_line[2])
    for i in range(4):
        bias_out[:, i * lanes:(i + 1) * lanes] = everything[i:i + 1] * factor
    plane_all, core_all = [], []
    for c in chunks:
        for copy in line_all[c]:
            copy.wait_recv()
        own_q = region(c, rep, q, 0, quarter)
        copies = {j: remote(own_q, own_q, pg_s.at[c, j], pg_r.at[c, j], plane_peer[j]) for j in (3, 1, 2)}
        for copy in copies.values():
            copy.start()
        plane_all.append(copies)
        core_all.append(remote(own_q, own_q, cg_s.at[c, 0], cg_r.at[c, 0], core_peer))
        core_all[-1].start()
    for c in chunks:
        for j in (1, 2, 3):
            plane_all[c][j].wait_recv()
            piece = region(c, rep, flip(j), 0, quarter)
            core_all.append(remote(piece, piece, cg_s.at[c, j], cg_r.at[c, j], core_peer))
            core_all[-1].start()
    for copy in core_all:
        copy.wait()
    store_wg = []
    for c in chunks:
        store_wg.append(pltpu.make_async_copy(fin.at[c], wg_out.at[:, pl.ds(c * columns, columns)], loc_sem.at[5 + c]))
        store_wg[-1].start()
    for copies in plane_sum + line_sum + line_all + [list(p.values()) for p in plane_all] + [pair]:
        for copy in copies:
            copy.wait_send()

    for c in sum(x_copy + y_copy, []) + dx_copy + dy_copy:
        c.wait_send()

    @pl.when(z < Z - 1)
    def _():
        for c in up:
            c.wait_send()

    @pl.when(z > 0)
    def _():
        for c in down:
            c.wait_send()

    @pl.when(middle)
    def _():
        for c in list(relay[0].values()) + list(relay[1].values()):
            c.wait_send()

    store_hid.wait()
    for copy in store_wg:
        copy.wait()


def fused_shards(features, col_panels, block_counts, block_values, weight, bias, cotangent):
    tile, width = features.shape
    bf16, f32 = jnp.bfloat16, jnp.float32
    half_rows, columns = width // 2, width // CHUNKS
    quarter = half_rows // PLANE
    share = quarter // Z
    dma = pltpu.SemaphoreType.DMA
    hbm = pl.BlockSpec(memory_space=pl.ANY)

    smem = pl.BlockSpec(memory_space=pltpu.SMEM)
    vmem = pl.BlockSpec(memory_space=pltpu.VMEM)
    factor = 1.0 / math.sqrt(lax.axis_size("section") * lax.axis_size("rep") * tile)
    hidden, weight_sum, bias_sum = pl.pallas_call(
        functools.partial(fused_kernel, factor),
        out_shape=(
            jax.ShapeDtypeStruct((tile, width), bf16),
            jax.ShapeDtypeStruct((width, width), bf16),
            jax.ShapeDtypeStruct((1, width), f32),
        ),
        in_specs=[hbm, smem, smem, hbm, hbm, vmem, hbm],
        out_specs=(hbm, hbm, vmem),
        scratch_shapes=[
            pltpu.VMEM((PLANE, Z * tile, width), bf16),
            pltpu.VMEM((PLANE, 2 * tile, Z * tile), bf16),
            pltpu.VMEM(block_values.shape, bf16),
            pltpu.VMEM((width, width), bf16),
            pltpu.VMEM((tile, width), bf16),
            pltpu.VMEM((tile, width), f32),
            pltpu.VMEM((tile, width), f32),
            pltpu.VMEM((tile, width), f32),
            pltpu.VMEM((tile, width), bf16),
            pltpu.VMEM((tile, width), bf16),
            pltpu.VMEM((CHUNKS, half_rows, columns), bf16),
            pltpu.VMEM((CHUNKS, half_rows, columns), bf16),
            pltpu.VMEM((CHUNKS, half_rows, columns), f32),
            pltpu.VMEM((CHUNKS, half_rows, columns), bf16),
            pltpu.VMEM((CHUNKS, 3, quarter, columns), bf16),
            pltpu.VMEM((CHUNKS, quarter, columns), f32),
            pltpu.VMEM((CHUNKS, quarter, columns), bf16),
            pltpu.VMEM((CHUNKS, 3, share, columns), bf16),
            pltpu.VMEM((CHUNKS, width, columns), bf16),
            pltpu.VMEM((3, 8, width // 4), f32),
            pltpu.VMEM((8, width // 4), f32),
            pltpu.VMEM((3, 8, width // 4), f32),
            pltpu.VMEM((3, 8, width // 4), f32),
            dma((5 + CHUNKS,)),
            dma((2, 5)), dma((2, 4)), dma((2, 4)), dma((2, 4)), dma((2, 4)), dma((2, 4)),
            dma((4,)), dma((4,)), dma((4,)), dma((4,)),
            dma((2 + CHUNKS,)), dma((2 + CHUNKS,)), dma((8,)), dma((8,)),
        ] + [dma((CHUNKS, 4))] * 10,
        compiler_params=pltpu.CompilerParams(
            collective_id=0, has_side_effects=True, vmem_limit_bytes=60 * 1024 * 1024
        ),
        name="fused_layer",
    )(features, col_panels, block_counts.reshape(-1), block_values, weight, bias.reshape(1, width), cotangent)
    return hidden, weight_sum.astype(f32) * factor, bias_sum[0]


def fits_fused(mesh):
    return dict(mesh.shape) == {"section": Z * PLANE, "rep": 2}


def solution(mesh):
    in_specs = (
        P(("section", "rep"), None),
        P("section", "rep", None),
        P("section", "rep"),
        P("section", "rep", None, None, None),
        P(),
        P(),
        P(("section", "rep"), None),
    )
    out_specs = (P(("section", "rep"), None), P(), P())
    body = fused_shards if fits_fused(mesh) else shards
    return jax.shard_map(body, mesh=mesh, in_specs=in_specs, out_specs=out_specs, check_vma=False)
```

```python
import functools
import math

import jax
import jax.numpy as jnp
from jax import lax
from jax.experimental import pallas as pl
from jax.experimental.pallas import tpu as pltpu
from jax.sharding import PartitionSpec as P


def shards(features, col_panels, block_counts, block_values, weight, bias, cotangent):
    rep_count = lax.axis_size("rep")
    rep_index = lax.axis_index("rep")
    tile_size = block_values.shape[-1]
    feat_width = features.shape[1]
    own_panels = features.shape[0] // tile_size
    row_panels = col_panels.shape[0]
    slot_count = col_panels.shape[2]
    global_cols = col_panels[:, 0, :]
    local_cols = global_cols // (own_panels * rep_count) * own_panels + global_cols % own_panels
    live_counts = block_counts[:, 0]
    slot_mask = jnp.arange(slot_count, dtype=jnp.int32)[None, :] < live_counts[:, None]
    tiles = block_values[:, 0]
    empty = jnp.zeros((row_panels, tile_size, feat_width), jnp.float32)
    gathered = lax.all_gather(features, "section", axis=0, tiled=True)
    all_panels = gathered.reshape(-1, tile_size, feat_width)
    slot_step = 4
    turn_count = (jnp.max(live_counts) + slot_step - 1) // slot_step

    def one_turn(turn, running):
        begin_slot = turn * slot_step
        step_cols = lax.dynamic_slice_in_dim(local_cols, begin_slot, slot_step, 1)
        step_mask = lax.dynamic_slice_in_dim(slot_mask, begin_slot, slot_step, 1)
        step_tiles = lax.dynamic_slice_in_dim(tiles, begin_slot, slot_step, 1)
        step_tiles = jnp.where(step_mask[:, :, None, None], step_tiles, jnp.zeros((), jnp.bfloat16))
        picked = all_panels[step_cols]
        return running + jnp.einsum(
            "gkab,gkbf->gaf", step_tiles, picked, preferred_element_type=jnp.float32
        )

    gathered_sum = lax.fori_loop(0, turn_count, one_turn, empty)
    partial_value = gathered_sum.reshape(row_panels * tile_size, feat_width)
    own_rows = own_panels * tile_size
    summed_all = lax.psum(partial_value, "rep")
    summed_own = lax.dynamic_slice_in_dim(summed_all, rep_index * own_rows, own_rows, 0)
    aggregated = summed_own.astype(jnp.bfloat16)
    pre = jnp.dot(aggregated, weight, preferred_element_type=jnp.float32) + bias
    hidden = jax.nn.silu(pre).astype(jnp.bfloat16)
    sigmoid_pre = jax.nn.sigmoid(pre)
    slope = (
        cotangent.astype(jnp.float32) * (sigmoid_pre * (1.0 + pre * (1.0 - sigmoid_pre)))
    ).astype(jnp.bfloat16)
    local_weight = jnp.einsum("nd,nf->df", aggregated, slope, preferred_element_type=jnp.float32)
    local_bias = jnp.sum(slope.astype(jnp.float32), axis=0)
    weight_sum, bias_sum = lax.psum((local_weight, local_bias), ("section", "rep"))
    node_total = lax.axis_size("section") * rep_count * own_rows
    factor = 1.0 / math.sqrt(node_total)
    return (hidden, weight_sum * factor, bias_sum * factor)

MESH = pl.DeviceIdType.MESH
Z, PLANE = 4, 4
CHUNKS = 4


def fused_kernel(
    factor,
    feat, cols, counts, blocks, weight, bias, cot,
    hid_out, wg_out, bias_out,
    gath, dense, blk, wv, cotv, acc_own, acc_oth, acc_in, aggs, hidv,
    pair_out, pair_in, half32, half16, plane_in, sum32, sum16, line_in, fin,
    ext, ext_pair, ext_plane, ext_line,
    loc_sem, z_s, z_r, x_s, x_r, y_s, y_r, dx_s, dx_r, dy_s, dy_r,
    p_s, p_r, e_s, e_r, rs_s, rs_r, zl_s, zl_r, zg_s, zg_r, pg_s, pg_r, cg_s, cg_r,
):
    tile, width = feat.shape
    me, rep = lax.axis_index("section"), lax.axis_index("rep")
    z, q = me // PLANE, me % PLANE
    y, x = q // 2, q % 2

    def flip(j):
        return (1 - y if j & 2 else y) * 2 + (1 - x if j & 1 else x)

    def line(d):
        return lax.rem(z + d, Z)

    plane_peer = {j: (z * PLANE + flip(j), rep) for j in (1, 2, 3)}
    line_peer = {d: (line(d) * PLANE + q, rep) for d in (1, 2, 3)}
    core_peer = (me, 1 - rep)

    def remote(src, dst, send, recv, peer):
        return pltpu.make_async_remote_copy(
            src_ref=src, dst_ref=dst, send_sem=send, recv_sem=recv,
            device_id=peer, device_id_type=MESH,
        )

    own = gath.at[0, pl.ds(0, tile)]
    load_feat = pltpu.make_async_copy(feat, own, loc_sem.at[0])
    load_blk = pltpu.make_async_copy(blocks, blk, loc_sem.at[1])
    load_w = pltpu.make_async_copy(weight, wv, loc_sem.at[2])
    load_cot = pltpu.make_async_copy(cot, cotv, loc_sem.at[3])
    for c in (load_feat, load_blk, load_w, load_cot):
        c.start()

    barrier = pltpu.get_barrier_semaphore()
    peers = list(plane_peer.values()) + list(line_peer.values()) + [core_peer]
    for peer in peers:
        pl.semaphore_signal(barrier, inc=1, device_id=peer, device_id_type=MESH)
    pl.semaphore_wait(barrier, len(peers))
    load_feat.wait()

    def slot(j, k):
        return gath.at[j, pl.ds(pl.multiple_of(k * tile, tile), tile)]

    def half(j, k, h):
        part = tile // 2
        return gath.at[j, pl.ds(pl.multiple_of(k * tile + h * part, part), part)]

    first = 1 + 2 * (z // 2)
    second = 2 + z - 3 * (z // 2)
    order = (0, first, second, 6 - first - second)
    middle = (z + 1) // 2 == 1

    def pass_on(i, h, target):
        k = order[i]
        there = lax.rem(z + k - target + Z, Z)
        return remote(half(0, k, h), half(0, there, h), z_s.at[h, i], z_r.at[h, there], (target * PLANE + q, rep))

    up = [remote(half(0, 0, h), half(0, Z - 1, h), z_s.at[h, 0], z_r.at[h, Z - 1], ((z + 1) * PLANE + q, rep)) for h in range(2)]
    down = [remote(half(0, 0, h), half(0, 1, h), z_s.at[h, 4], z_r.at[h, 1], ((z - 1) * PLANE + q, rep)) for h in range(2)]
    outer, inner = lax.rem(3 * z + 1, Z), Z - 1 - z
    relay = [{1: pass_on(1, h, outer), 2: pass_on(2, h, inner), 3: pass_on(3, h, outer)} for h in range(2)]

    def across(j, i, h):
        k = order[i]
        send, recv = ((x_s, x_r), (y_s, y_r))[j - 1]
        return remote(half(0, k, h), half(j, k, h), send.at[h, k], recv.at[h, k], plane_peer[j])

    x_copy = [[across(1, i, h) for h in range(2)] for i in range(Z)]
    y_copy = [[across(2, i, h) for h in range(2)] for i in range(Z)]
    for h in range(2):
        x_copy[0][1 - h].start()
        y_copy[0][h].start()

        @pl.when(z < Z - 1)
        def _():
            up[h].start()

        @pl.when(z > 0)
        def _():
            down[h].start()

    dx_copy = [remote(half(2, k, 0), half(3, k, 0), dx_s.at[k], dx_r.at[k], plane_peer[1]) for k in order]
    dy_copy = [remote(half(1, k, 1), half(3, k, 1), dy_s.at[k], dy_r.at[k], plane_peer[2]) for k in order]
    def live(p):
        panel = rep if p == 0 else 1 - rep
        count = counts[panel]
        return [jnp.where(s < count, cols[panel, 0, s], -1) for s in range(cols.shape[2])]

    lists = [live(0), live(1)]
    load_blk.wait()
    for j in range(PLANE):
        for k in range(Z):
            for p in range(2):
                panel = rep if p == 0 else 1 - rep
                column = (line(k) * PLANE + flip(j)) * 2 + rep
                place = jnp.int32(0)
                for s, listed in enumerate(lists[p]):
                    place = jnp.where(listed == column, jnp.int32(s + 1), place)
                block = blk[panel, 0, jnp.maximum(place - 1, 0)]
                keep = jnp.minimum(place, 1).astype(jnp.float32).astype(jnp.bfloat16)
                dense[j, pl.ds(p * tile, tile), pl.ds(k * tile, tile)] = block * keep

    def forward(i):
        x_copy[i][1].wait_recv()
        dy_copy[i].start()
        y_copy[i][0].wait_recv()
        dx_copy[i].start()

    for i in (1, 2, 3):
        for h in range(2):
            k = order[i]
            pltpu.make_async_copy(half(0, 0, h), half(0, k, h), z_r.at[h, k]).wait()

            @pl.when(middle)
            def _():
                relay[h][i].start()

            (y_copy if h == 0 else x_copy)[i][h].start()
        x_copy[i][0].start()
        y_copy[i][1].start()
        forward(i - 1)
    mine, theirs = pl.ds(0, tile), pl.ds(tile, tile)

    def product(j, part):
        return jnp.dot(dense[j, part], gath[j], preferred_element_type=jnp.float32)

    def corner(i, part):
        at = pl.ds(pl.multiple_of(order[i] * tile, tile), tile)
        return jnp.dot(dense[3, part, at], gath[3, at], preferred_element_type=jnp.float32)

    acc_own[...] = product(0, mine)
    acc_oth[...] = product(0, theirs)
    forward(3)
    for i in range(Z):
        x_copy[i][0].wait_recv()
        y_copy[i][1].wait_recv()
    for j in (1, 2):
        acc_own[...] += product(j, mine)
        acc_oth[...] += product(j, theirs)
    for i in range(Z):
        dx_copy[i].wait_recv()
        dy_copy[i].wait_recv()
        acc_oth[...] += corner(i, theirs)
        if i < Z - 1:
            acc_own[...] += corner(i, mine)
    swap = remote(acc_oth, acc_in, p_s.at[0], p_r.at[0], core_peer)
    swap.start()
    acc_own[...] += corner(Z - 1, mine)
    load_w.wait()
    load_cot.wait()
    swap.wait()

    agg = (acc_own[...] + acc_in[...]).astype(jnp.bfloat16)
    aggs[...] = agg
    pre = jnp.dot(agg, wv[...], preferred_element_type=jnp.float32) + bias[...]
    sig = jax.nn.sigmoid(pre)
    slope = (cotv[...].astype(jnp.float32) * (sig * (1.0 + pre * (1.0 - sig)))).astype(jnp.bfloat16)
    half_rows, columns = width // 2, width // CHUNKS
    quarter = half_rows // PLANE
    share = quarter // Z
    aligned = pl.multiple_of

    def grad_half(which, c):
        part = aggs[:, pl.ds(aligned(which * half_rows, half_rows), half_rows)]
        cut = slope[:, c * columns:(c + 1) * columns]
        return lax.dot_general(part, cut, (((0,), (0,)), ((), ())), preferred_element_type=jnp.float32)

    chunks = range(CHUNKS)
    pair = [remote(pair_out.at[c], pair_in.at[c], p_s.at[c + 2], p_r.at[c + 2], core_peer) for c in chunks]
    for c in chunks:
        pair_out[c] = grad_half(1 - rep, c).astype(jnp.bfloat16)
        pair[c].start()
    total = jnp.sum(slope.astype(jnp.float32), axis=0, keepdims=True)
    lanes = width // 4
    row_id = lax.broadcasted_iota(jnp.int32, (8, lanes), 0)
    spread = jnp.zeros((8, lanes), jnp.float32)
    for i in range(4):
        spread = jnp.where(row_id == i, total[:, i * lanes:(i + 1) * lanes], spread)
    ext[0] = spread
    ext_copy = remote(ext.at[0], ext_pair, p_s.at[1], p_r.at[1], core_peer)
    ext_copy.start()

    plane_sum = []
    for c in chunks:
        own_half = grad_half(rep, c)
        pair[c].wait_recv()
        both = own_half + pair_in[c].astype(jnp.float32)
        half32[c] = both
        half16[c] = both.astype(jnp.bfloat16)
        copies = []
        for j in (3, 1, 2):
            piece = half16.at[c, pl.ds(aligned(flip(j) * quarter, quarter), quarter)]
            copies.append(remote(piece, plane_in.at[c, j - 1], rs_s.at[c, j], rs_r.at[c, j], plane_peer[j]))
        for copy in copies:
            copy.start()
        plane_sum.append(copies)
    ext_copy.wait()
    ext[1] = ext[0] + ext_pair[...]
    ext_sum = [remote(ext.at[1], ext_plane.at[j - 1], e_s.at[j], e_r.at[j], plane_peer[j]) for j in (1, 2, 3)]
    for copy in ext_sum:
        copy.start()
    hidv[...] = (pre * sig).astype(jnp.bfloat16)
    store_hid = pltpu.make_async_copy(hidv, hid_out, loc_sem.at[4])
    store_hid.start()

    line_sum = []
    for c in chunks:
        for copy in plane_sum[c]:
            copy.wait_recv()
        part = half32[c, pl.ds(aligned(q * quarter, quarter), quarter)]
        for j in range(3):
            part = part + plane_in[c, j].astype(jnp.float32)
        sum32[c] = part
        sum16[c] = part.astype(jnp.bfloat16)
        copies = []
        for d in (2, 1, 3):
            piece = sum16.at[c, pl.ds(aligned(line(d) * share, share), share)]
            copies.append(remote(piece, line_in.at[c, Z - d - 1], zl_s.at[c, d], zl_r.at[c, Z - d], line_peer[d]))
        for copy in copies:
            copy.start()
        line_sum.append(copies)
    for copy in ext_sum:
        copy.wait()
    ext[2] = ext[1] + (ext_plane[0] + ext_plane[1] + ext_plane[2])
    ext_line_sum = [remote(ext.at[2], ext_line.at[Z - d - 1], e_s.at[d + 4], e_r.at[Z - d + 4], line_peer[d]) for d in (1, 2, 3)]
    for copy in ext_line_sum:
        copy.start()

    def region(c, core, place, height, count):
        start = core * half_rows + place * quarter + height * share
        return fin.at[c, pl.ds(aligned(start, share), count)]

    line_all = []
    for c in chunks:
        for copy in line_sum[c]:
            copy.wait_recv()
        part = sum32[c, pl.ds(aligned(z * share, share), share)]
        for d in range(3):
            part = part + line_in[c, d].astype(jnp.float32)
        here = region(c, rep, q, z, share)
        here[...] = part.astype(jnp.bfloat16)
        copies = [remote(here, here, zg_s.at[c, d], zg_r.at[c, Z - d], line_peer[d]) for d in (2, 1, 3)]
        for copy in copies:
            copy.start()
        line_all.append(copies)
    for copy in ext_line_sum:
        copy.wait()
    everything = ext[2] + (ext_line[0] + ext_line[1] + ext_line[2])
    for i in range(4):
        bias_out[:, i * lanes:(i + 1) * lanes] = everything[i:i + 1] * factor
    plane_all, core_all = [], []
    for c in chunks:
        for copy in line_all[c]:
            copy.wait_recv()
        own_q = region(c, rep, q, 0, quarter)
        copies = {j: remote(own_q, own_q, pg_s.at[c, j], pg_r.at[c, j], plane_peer[j]) for j in (3, 1, 2)}
        for copy in copies.values():
            copy.start()
        plane_all.append(copies)
        core_all.append(remote(own_q, own_q, cg_s.at[c, 0], cg_r.at[c, 0], core_peer))
        core_all[-1].start()
    for c in chunks:
        for j in (1, 2, 3):
            plane_all[c][j].wait_recv()
            piece = region(c, rep, flip(j), 0, quarter)
            core_all.append(remote(piece, piece, cg_s.at[c, j], cg_r.at[c, j], core_peer))
            core_all[-1].start()
    for copy in core_all:
        copy.wait()
    store_wg = []
    for c in chunks:
        store_wg.append(pltpu.make_async_copy(fin.at[c], wg_out.at[:, pl.ds(c * columns, columns)], loc_sem.at[5 + c]))
        store_wg[-1].start()
    for copies in plane_sum + line_sum + line_all + [list(p.values()) for p in plane_all] + [pair]:
        for copy in copies:
            copy.wait_send()

    for c in sum(x_copy + y_copy, []) + dx_copy + dy_copy:
        c.wait_send()

    @pl.when(z < Z - 1)
    def _():
        for c in up:
            c.wait_send()

    @pl.when(z > 0)
    def _():
        for c in down:
            c.wait_send()

    @pl.when(middle)
    def _():
        for c in list(relay[0].values()) + list(relay[1].values()):
            c.wait_send()

    store_hid.wait()
    for copy in store_wg:
        copy.wait()


def fused_shards(features, col_panels, block_counts, block_values, weight, bias, cotangent):
    tile, width = features.shape
    bf16, f32 = jnp.bfloat16, jnp.float32
    half_rows, columns = width // 2, width // CHUNKS
    quarter = half_rows // PLANE
    share = quarter // Z
    dma = pltpu.SemaphoreType.DMA
    hbm = pl.BlockSpec(memory_space=pl.ANY)

    smem = pl.BlockSpec(memory_space=pltpu.SMEM)
    vmem = pl.BlockSpec(memory_space=pltpu.VMEM)
    factor = 1.0 / math.sqrt(lax.axis_size("section") * lax.axis_size("rep") * tile)
    hidden, weight_sum, bias_sum = pl.pallas_call(
        functools.partial(fused_kernel, factor),
        out_shape=(
            jax.ShapeDtypeStruct((tile, width), bf16),
            jax.ShapeDtypeStruct((width, width), bf16),
            jax.ShapeDtypeStruct((1, width), f32),
        ),
        in_specs=[hbm, smem, smem, hbm, hbm, vmem, hbm],
        out_specs=(hbm, hbm, vmem),
        scratch_shapes=[
            pltpu.VMEM((PLANE, Z * tile, width), bf16),
            pltpu.VMEM((PLANE, 2 * tile, Z * tile), bf16),
            pltpu.VMEM(block_values.shape, bf16),
            pltpu.VMEM((width, width), bf16),
            pltpu.VMEM((tile, width), bf16),
            pltpu.VMEM((tile, width), f32),
            pltpu.VMEM((tile, width), f32),
            pltpu.VMEM((tile, width), f32),
            pltpu.VMEM((tile, width), bf16),
            pltpu.VMEM((tile, width), bf16),
            pltpu.VMEM((CHUNKS, half_rows, columns), bf16),
            pltpu.VMEM((CHUNKS, half_rows, columns), bf16),
            pltpu.VMEM((CHUNKS, half_rows, columns), f32),
            pltpu.VMEM((CHUNKS, half_rows, columns), bf16),
            pltpu.VMEM((CHUNKS, 3, quarter, columns), bf16),
            pltpu.VMEM((CHUNKS, quarter, columns), f32),
            pltpu.VMEM((CHUNKS, quarter, columns), bf16),
            pltpu.VMEM((CHUNKS, 3, share, columns), bf16),
            pltpu.VMEM((CHUNKS, width, columns), bf16),
            pltpu.VMEM((3, 8, width // 4), f32),
            pltpu.VMEM((8, width // 4), f32),
            pltpu.VMEM((3, 8, width // 4), f32),
            pltpu.VMEM((3, 8, width // 4), f32),
            dma((5 + CHUNKS,)),
            dma((2, 5)), dma((2, 4)), dma((2, 4)), dma((2, 4)), dma((2, 4)), dma((2, 4)),
            dma((4,)), dma((4,)), dma((4,)), dma((4,)),
            dma((2 + CHUNKS,)), dma((2 + CHUNKS,)), dma((8,)), dma((8,)),
        ] + [dma((CHUNKS, 4))] * 10,
        compiler_params=pltpu.CompilerParams(
            collective_id=0, has_side_effects=True, vmem_limit_bytes=60 * 1024 * 1024
        ),
        name="fused_layer",
    )(features, col_panels, block_counts.reshape(-1), block_values, weight, bias.reshape(1, width), cotangent)
    return hidden, weight_sum.astype(f32) * factor, bias_sum[0]


def fits_fused(mesh):
    return dict(mesh.shape) == {"section": Z * PLANE, "rep": 2}


def solution(mesh):
    in_specs = (
        P(("section", "rep"), None),
        P("section", "rep", None),
        P("section", "rep"),
        P("section", "rep", None, None, None),
        P(),
        P(),
        P(("section", "rep"), None),
    )
    out_specs = (P(("section", "rep"), None), P(), P())
    body = fused_shards if fits_fused(mesh) else shards
    return jax.shard_map(body, mesh=mesh, in_specs=in_specs, out_specs=out_specs, check_vma=False)
```
